256 devices in a mesh: gx: 16 (over z_lo, y, core), gy: 16 (over x, z_hi).
Axes of the slice: x: 4, y: 4, z: 8 (z_hi: 4, z_lo: 2; z = z_hi * 2 + z_lo), core: 2. Of those that a mesh axis runs over, the one named last changes fastest.
Arguments:
- field: float32 [1, 20, 128, 128, 768], P(None, None, 'gx', 'gy'), may hold values from -6 to 6
- spec_weight: float32 [20, 20, 24, 9216], P(None, None, None, ('gx', 'gy')), may hold values from -2.5 to 2.5
- bypass_weight: float32 [20, 20], replicated, may hold values from -1.25 to 1.25
- bypass_bias: float32 [20], replicated, may hold values from -3 to 3
Outputs:
- activated: float32 [1, 20, 128, 128, 768], P(None, None, 'gx', 'gy')
The draws below stay inside these ranges and needn't reach their ends.
All inputs are finite; a program needn't handle non-finite values.
Results may differ from the reference program's by a relative error of at most 0.00005.
Values sent between devices are 32-bit elements; how exact they have to be, the bound alone decides.
No kernel may reach another device: no remote copies, remote signals or barrier semaphores. Data moves between devices by JAX's collectives and lax.ppermute only.
A program may use at most 128 MiB of HBM per device.

```python
from functools import partial
import jax
import jax.numpy as jnp
from jax import lax

B = 1
C = 20
NZ = 32
NT = 24
KX = 24
KY = 24
KZ = 16
KT = 12
NX = 128
NY = 128
ZT = 768
MZT = 192


def shard_levels(stream_key, dims, shards, least, high):
    factor_of, own = 1.0, jax.random.fold_in(stream_key, 6)
    for dim, parts in shards:
        heights = jnp.exp(jax.random.uniform(jax.random.fold_in(own, dim), (parts,), jnp.float32, least / len(shards), high / len(shards)))
        factor_of = factor_of * jnp.repeat(heights, dims[dim] // parts).reshape([-1 if axis == dim else 1 for axis in range(len(dims))])
    return factor_of


def bell_draw(own_key, extent, spread, reach, shards=(), kind=jnp.bfloat16):
    gain = shard_levels(own_key, extent, shards, -0.22, 0.18) if shards else 1.0
    array = jax.random.normal(own_key, extent, jnp.float32) * spread * gain
    return jnp.minimum(jnp.maximum(array, -reach), reach).astype(kind)


def setup_inputs(seed: int = 0) -> dict:
    streams_of = jax.random.split(jax.random.key(seed), 5)
    field = bell_draw(streams_of[0], (B, C, NX, NY, ZT), 1.0, 6.0, ((2, 16), (3, 16)), jnp.float32)
    spec_weight = bell_draw(streams_of[1], (C, C, KY, 2 * MZT * KX), (C // 4) ** -0.5, 2.5, ((3, 256),), jnp.float32)
    bypass_weight = bell_draw(streams_of[2], (C, C), C ** -0.5, 1.25, (), jnp.float32)
    bypass_bias = bell_draw(streams_of[3], (C,), 0.5, 3.0, (), jnp.float32)
    return dict(field=field, spec_weight=spec_weight, bypass_weight=bypass_weight, bypass_bias=bypass_bias)


def kept_index(count, length):
    steps = jnp.arange(count, dtype=jnp.int32)
    return jnp.where(steps < count // 2, steps, length - count + steps).astype(jnp.int32)


def reference(field, spec_weight, bypass_weight, bypass_bias):
    contract = partial(jnp.einsum, precision=lax.Precision.HIGHEST)
    x_index = kept_index(KX, NX)
    y_index = kept_index(KY, NY)
    z_index = kept_index(KZ, NZ)
    t_index = jnp.arange(KT, dtype=jnp.int32)
    cube = field.reshape(B * C, NX, NY, NZ, NT)

    def forward(block):
        spectrum = jnp.fft.rfftn(block)
        spectrum = spectrum[x_index][:, y_index][:, :, z_index][:, :, :, :KT]
        return jnp.stack([jnp.real(spectrum), jnp.imag(spectrum)])

    coeffs = lax.map(forward, cube).reshape(B, C, 2, KX, KY, KZ, KT)
    weights = spec_weight.reshape(C, C, KY, KZ, KT, KX, 2)
    weights = jnp.transpose(weights, (6, 0, 1, 5, 2, 3, 4))
    coef_real = coeffs[:, :, 0]
    coef_imag = coeffs[:, :, 1]
    form = 'bixyzt,ioxyzt->boxyzt'
    mixed_real = contract(form, coef_real, weights[0]) - contract(form, coef_imag, weights[1])
    mixed_imag = contract(form, coef_real, weights[1]) + contract(form, coef_imag, weights[0])

    def inverse(pair):
        spectrum = lax.complex(pair[0], pair[1])
        full = jnp.zeros((NX, NY, NZ, NT // 2 + 1), spectrum.dtype)
        full = full.at[x_index[:, None, None, None], y_index[None, :, None, None],
                       z_index[None, None, :, None], t_index[None, None, None, :]].set(spectrum)
        return jnp.fft.irfftn(full, s=(NX, NY, NZ, NT)).reshape(NX, NY, NZ * NT)

    spectral = lax.map(inverse, (mixed_real.reshape(B * C, KX, KY, KZ, KT),
                                 mixed_imag.reshape(B * C, KX, KY, KZ, KT)))
    spectral = spectral.reshape(B, C, NX, NY, NZ * NT)
    bypass = contract('oi,bixyn->boxyn', bypass_weight, field) + bypass_bias[None, :, None, None, None]
    return jax.nn.gelu(spectral + bypass, approximate=False)
```

```python
import jax
import jax.numpy as jnp
import ml_dtypes
import numpy as np
from jax import lax
from jax.experimental import pallas as pl
from jax.experimental.pallas import tpu as pltpu
from jax.sharding import PartitionSpec as P

C, NX, NY, NZ, NT = 20, 128, 128, 32, 24
KX, KY, KZ, KT = 24, 24, 16, 12
ZT, MZT = NZ * NT, KZ * KT
GX = GY = 16
RX, RY = NX // GX, NY // GY
BM = MZT // GX
H = BM * KX // GY
HQ = 2 * H
CM, CR = 16, 4
MAIN = BM * 2 * RX
ROWS = MAIN + BM * 2 * RX * CR // CM
LANES = 768
MIB = 1024 * 1024

NN = (((1,), (0,)), ((), ()))
NT_DIMS = (((1,), (1,)), ((), ()))


def slot_mode(slot):
    return (slot % 4) * 3 + slot // 4


def kept(count, length):
    steps = np.arange(count)
    return np.where(steps < count // 2, steps, length - count + steps)


def halves(table):
    table = table.astype(np.float32)
    high = table.astype(ml_dtypes.bfloat16)
    low = (table - high.astype(np.float32)).astype(ml_dtypes.bfloat16)
    return np.stack([high, low])


def depth_tables():
    kz = kept(KZ, NZ)
    modes = np.array([g * BM + slot_mode(s) for g in range(GX) for s in range(BM)])
    z_freq, t_freq = kz[modes // KT], modes % KT
    cells = np.arange(ZT)
    turns = (z_freq[:, None] * (cells // NT)[None] * NT + t_freq[:, None] * (cells % NT)[None] * NZ) % ZT
    angle = turns * (2.0 * np.pi / ZT)
    cosine, sine = np.cos(angle), np.sin(angle)
    forward = np.stack([cosine, -sine], axis=1).reshape(2 * MZT, ZT)
    scale = (np.where(t_freq == 0, 1.0, 2.0) / (NX * NY * ZT))[:, None]
    inverse = np.stack([cosine * scale, -sine * scale], axis=1).reshape(2 * MZT, ZT)
    return halves(forward), halves(inverse)


def x_tables():
    angle = (np.arange(NX)[:, None] * kept(KX, NX)[None] % NX) * (2.0 * np.pi / NX)
    cosine, sine = np.cos(angle), np.sin(angle)
    forward = np.stack([np.stack([cosine, -sine], -1), np.stack([sine, cosine], -1)], 1)
    back = np.stack([np.stack([cosine, -sine], -1), np.stack([sine, cosine], -1)], 1)
    shape = (GX, RX, 2, KX * 2)
    forward, back = forward.reshape(shape), back.reshape(shape)
    def main(table):
        return table.transpose(0, 2, 1, 3).reshape(GX * 2 * RX, KX * 2)
    def rest(table):
        return table.reshape(GX * RX * 2, KX * 2)
    return (
        np.stack([halves(main(forward).T), halves(rest(forward).T)]),
        np.stack([halves(main(back)), halves(rest(back))]),
    )


def y_tables():
    angle = (np.arange(NY)[:, None] * kept(KY, NY)[None] % NY) * (2.0 * np.pi / NY)
    cosine, sine = np.cos(angle), np.sin(angle)
    both = np.concatenate([cosine, sine], axis=1)
    return halves(both.T), halves(both)


def split(value):
    high = value.astype(jnp.bfloat16)
    return high, (value - high.astype(jnp.float32)).astype(jnp.bfloat16)


def product(left, right, dims):
    def term(a, b):
        return lax.dot_general(a, b, dims, preferred_element_type=jnp.float32)
    return term(left[0], right[0]) + (term(left[0], right[1]) + term(left[1], right[0]))


def block_swap(value):
    row = lax.broadcasted_iota(jnp.int32, value.shape, 1) // 2
    lane = lax.broadcasted_iota(jnp.int32, value.shape, 2) // 32
    far = pltpu.roll(pltpu.roll(value, 4, 1), 64, 2)
    value = jnp.where((row // 2) == (lane // 2), value, far)
    up = pltpu.roll(pltpu.roll(value, 6, 1), 32, 2)
    down = pltpu.roll(pltpu.roll(value, 2, 1), 96, 2)
    return jnp.where((row % 2) == (lane % 2), value, jnp.where(row % 2 == 0, up, down))


def depth_kernel(field, table, out):
    half = pl.program_id(0)
    tables = (table[0], table[1])
    for pair in range(2):
        cells = jnp.concatenate(
            [field[0:CM, 2 * pair + k].reshape(CM * RY, ZT) for k in range(2)], axis=0
        )
        modes = product(tables, split(cells), NT_DIMS)
        for k in range(2):
            for dest in range(GX):
                start = dest * ROWS + 2 * pair + k + half * 4
                out[pl.ds(start, 2 * BM, stride=RX), :] = modes[
                    dest * 2 * BM : (dest + 1) * 2 * BM, k * 128 : (k + 1) * 128
                ]
    cells = jnp.concatenate([field[CM:C, k].reshape(CR * RY, ZT) for k in range(4)], axis=0)
    modes = product(tables, split(cells), NT_DIMS)
    tiles = block_swap(modes.reshape(GX * 3, 8, 128))
    for dest in range(GX):
        for third in range(3):
            start = pl.multiple_of(dest * ROWS + MAIN + third * 16 + half * 8, 8)
            out[pl.ds(start, 8), :] = tiles[dest * 3 + third]


def depth_transform(field, table):
    return pl.pallas_call(
        depth_kernel,
        grid=(2,),
        in_specs=[
            pl.BlockSpec((C, 4, RY, ZT), lambda i: (0, i, 0, 0)),
            pl.BlockSpec((2, 2 * MZT, ZT), lambda i: (0, 0, 0)),
        ],
        out_specs=pl.BlockSpec((GX * ROWS, 128), lambda i: (0, 0)),
        out_shape=jax.ShapeDtypeStruct((GX * ROWS, 128), jnp.float32),
        compiler_params=pltpu.CompilerParams(vmem_limit_bytes=40 * MIB),
        cost_estimate=pl.CostEstimate(flops=2300000000, bytes_accessed=7000000, transcendentals=0),
        name="depth_forward",
    )(field, table)


def x_kernel(cells, table, out, held):
    main_table = (table[0, 0], table[0, 1])
    rest_table = (table[1, 0], table[1, 1])
    for slot in range(BM):
        columns = jnp.concatenate(
            [cells[pl.ds(s * ROWS + slot * 16, 16), :] for s in range(GX)], axis=0
        )
        mode = slot_mode(slot)
        held[pl.ds(mode * 2 * KX, 2 * KX), :] = product(main_table, split(columns), NN)
    for third in range(3):
        columns = jnp.concatenate(
            [cells[pl.ds(s * ROWS + MAIN + third * 16, 16), :] for s in range(GX)], axis=0
        )
        held[pl.ds((BM + third) * 2 * KX, 2 * KX), :] = product(rest_table, split(columns), NN)
    for g in range(GY):
        turned = held[pl.ds(g * HQ, HQ), :].T
        for c in range(CM):
            out[g, :, c * HQ : (c + 1) * HQ] = turned[c * RY : (c + 1) * RY]
    for b in range(4):
        turned = held[pl.ds(BM * 2 * KX + b * HQ, HQ), :].T
        for a in range(4):
            for c in range(CR):
                row = (a * CR + c) * RY
                out[4 * a + b, :, (CM + c) * HQ : (CM + c + 1) * HQ] = turned[row : row + RY]
    for g in range(GY):
        out[g, :, C * HQ : LANES] = jnp.zeros((RY, LANES - C * HQ), jnp.float32)


def x_transform(cells, table):
    return pl.pallas_call(
        x_kernel,
        out_shape=jax.ShapeDtypeStruct((GY, RY, LANES), jnp.float32),
        scratch_shapes=[pltpu.VMEM(((BM + 3) * 2 * KX, 128), jnp.float32)],
        compiler_params=pltpu.CompilerParams(vmem_limit_bytes=40 * MIB),
        cost_estimate=pl.CostEstimate(flops=150000000, bytes_accessed=2500000, transcendentals=0),
        name="x_forward",
    )(cells, table)


def even_lanes(shape):
    return lax.broadcasted_iota(jnp.int32, shape, len(shape) - 1) % 2 == 0


def turn_parts(value, even):
    lanes = value.shape[-1]
    return jnp.where(even, -pltpu.roll(value, lanes - 1, 1), pltpu.roll(value, 1, 1))


def mix_kernel(cells, weights, forward, back, out, reals, imags, mixed):
    sums = product((forward[0], forward[1]), split(cells[...].reshape(GY * RY, LANES)), NN)
    even = even_lanes((KY, LANES))
    coef = sums[:KY] - turn_parts(sums[KY:], even)
    real = jnp.where(even, coef, pltpu.roll(coef, 1, 1))
    imag = jnp.where(even, pltpu.roll(coef, LANES - 1, 1), coef)
    for i in range(C):
        reals[i] = real[:, i * HQ : (i + 1) * HQ]
        imags[i] = imag[:, i * HQ : (i + 1) * HQ]
    even_pairs = even_lanes((KY, HQ))
    group = 4
    for first in range(0, C, group):
        one = [jnp.zeros((KY, HQ), jnp.float32)] * group
        two = [jnp.zeros((KY, HQ), jnp.float32)] * group
        for i in range(C):
            real_i, imag_i = reals[i], imags[i]
            for k in range(group):
                weight = weights[i, first + k]
                one[k] = one[k] + weight * real_i
                two[k] = two[k] + weight * imag_i
        for k in range(group):
            o = first + k
            mixed[:, o * HQ : (o + 1) * HQ] = one[k] + turn_parts(two[k], even_pairs)
    mixed[:, C * HQ : LANES] = jnp.zeros((KY, LANES - C * HQ), jnp.float32)
    modes = mixed[...]
    both = jnp.concatenate([modes, turn_parts(modes, even)], axis=0)
    out[...] = product((back[0], back[1]), split(both), NN).reshape(GY, RY, LANES)


def mix_modes(cells, weights, forward, back):
    return pl.pallas_call(
        mix_kernel,
        out_shape=jax.ShapeDtypeStruct((GY, RY, LANES), jnp.float32),
        scratch_shapes=[
            pltpu.VMEM((C, KY, HQ), jnp.float32),
            pltpu.VMEM((C, KY, HQ), jnp.float32),
            pltpu.VMEM((KY, LANES), jnp.float32),
        ],
        compiler_params=pltpu.CompilerParams(vmem_limit_bytes=40 * MIB),
        cost_estimate=pl.CostEstimate(flops=60000000, bytes_accessed=6000000, transcendentals=0),
        name="y_mix",
    )(cells, weights, forward, back)


def x_back_kernel(modes, table, out, held):
    main_table = (table[0, 0], table[0, 1])
    rest_table = (table[1, 0], table[1, 1])
    for g in range(GY):
        rows = jnp.concatenate([modes[g, :, c * HQ : (c + 1) * HQ] for c in range(CM)], axis=0)
        held[pl.ds(g * HQ, HQ), :] = rows.T
    for b in range(4):
        rows = jnp.concatenate(
            [
                modes[4 * a + b, :, (CM + c) * HQ : (CM + c + 1) * HQ]
                for a in range(4)
                for c in range(CR)
            ],
            axis=0,
        )
        held[pl.ds(BM * 2 * KX + b * HQ, HQ), :] = rows.T
    for slot in range(BM):
        mode = slot_mode(slot)
        columns = held[pl.ds(mode * 2 * KX, 2 * KX), :]
        cells = product(main_table, split(columns), NN)
        for s in range(GX):
            out[pl.ds(s * ROWS + slot * 16, 16), :] = cells[s * 16 : (s + 1) * 16]
    for third in range(3):
        columns = held[pl.ds((BM + third) * 2 * KX, 2 * KX), :]
        cells = product(rest_table, split(columns), NN)
        for s in range(GX):
            out[pl.ds(s * ROWS + MAIN + third * 16, 16), :] = cells[s * 16 : (s + 1) * 16]


def x_back(modes, table):
    return pl.pallas_call(
        x_back_kernel,
        out_shape=jax.ShapeDtypeStruct((GX * ROWS, 128), jnp.float32),
        scratch_shapes=[pltpu.VMEM(((BM + 3) * 2 * KX, 128), jnp.float32)],
        compiler_params=pltpu.CompilerParams(vmem_limit_bytes=40 * MIB),
        cost_estimate=pl.CostEstimate(flops=150000000, bytes_accessed=2500000, transcendentals=0),
        name="x_back",
    )(modes, table)


def final_kernel(field, cells, table, channel_map, bias, out, rest):
    step = pl.program_id(0)
    tables = (table[0], table[1])
    maps = (channel_map[0], channel_map[1])

    @pl.when(step % 2 == 0)
    def _():
        tiles = jnp.stack(
            [
                cells[pl.ds(pl.multiple_of(s * ROWS + MAIN + third * 16 + (step // 2) * 8, 8), 8), :]
                for s in range(GX)
                for third in range(3)
            ]
        )
        rest[...] = block_swap(tiles).reshape(2 * MZT, 128).T

    columns = []
    for k in range(2):
        main = jnp.concatenate(
            [cells[pl.ds(s * ROWS + 2 * step + k, 2 * BM, stride=RX), :] for s in range(GX)], axis=0
        ).T
        row = pl.multiple_of(((step % 2) * 2 + k) * CR * RY, CR * RY)
        columns += [main, rest[pl.ds(row, CR * RY), :]]
    spectral = product(split(jnp.concatenate(columns, axis=0)), tables, NN)
    for k in range(2):
        bypass = product(maps, split(field[:, k].reshape(C * RY, ZT)), NN)
        value = spectral[k * C * RY : (k + 1) * C * RY] + bypass + bias[:, 0:1]
        value = 0.5 * value * (1.0 + lax.erf(value * np.float32(np.sqrt(0.5))))
        out[:, k] = value.reshape(C, RY, ZT)


def final_stage(field, cells, table, channel_map, bias):
    return pl.pallas_call(
        final_kernel,
        grid=(4,),
        in_specs=[
            pl.BlockSpec((C, 2, RY, ZT), lambda i: (0, i, 0, 0)),
            pl.BlockSpec((GX * ROWS, 128), lambda i: (0, 0)),
            pl.BlockSpec((2, 2 * MZT, ZT), lambda i: (0, 0, 0)),
            pl.BlockSpec((2, C * RY, C * RY), lambda i: (0, 0, 0)),
            pl.BlockSpec((C * RY, 128), lambda i: (0, 0)),
        ],
        out_specs=pl.BlockSpec((C, 2, RY, ZT), lambda i: (0, i, 0, 0)),
        out_shape=jax.ShapeDtypeStruct((C, RX, RY, ZT), jnp.float32),
        scratch_shapes=[pltpu.VMEM((128, 2 * MZT), jnp.float32)],
        compiler_params=pltpu.CompilerParams(vmem_limit_bytes=40 * MIB),
        cost_estimate=pl.CostEstimate(flops=3200000000, bytes_accessed=11000000, transcendentals=1000000),
        name="depth_back",
    )(field, cells, table, channel_map, bias)


def exchange(value, axis):
    return lax.all_to_all(value, axis, split_axis=0, concat_axis=0, tiled=True)


def shards(field, spec_weight, bypass_weight, bypass_bias):
    depth_forward, depth_back = depth_tables()
    x_forward, x_inverse = x_tables()
    y_forward, y_inverse = y_tables()
    field = field.reshape(C, RX, RY, ZT)
    spread = jnp.kron(bypass_weight, jnp.eye(RY, dtype=jnp.float32))
    spread_high = lax.reduce_precision(spread, 8, 7)
    channel_map = jnp.stack([spread_high, spread - spread_high]).astype(jnp.bfloat16)
    bias = jnp.broadcast_to(jnp.repeat(bypass_bias, RY)[:, None], (C * RY, 128))

    modes = depth_transform(field, depth_forward)
    cells = exchange(modes.reshape(GX, ROWS, 128), "gx").reshape(GX * ROWS, 128)
    pairs = exchange(x_transform(cells, x_forward), "gy")
    mixed = exchange(mix_modes(pairs, spec_weight, y_forward, y_inverse), "gy")
    back = x_back(mixed, x_inverse)
    back = exchange(back.reshape(GX, ROWS, 128), "gx").reshape(GX * ROWS, 128)
    out = final_stage(field, back, depth_back, channel_map, bias)
    return out.reshape(1, C, RX, RY, ZT)


def solution(mesh):
    in_specs = (P(None, None, "gx", "gy", None), P(None, None, None, ("gx", "gy")), P(), P())
    out_specs = P(None, None, "gx", "gy", None)
    return jax.shard_map(shards, mesh=mesh, in_specs=in_specs, out_specs=out_specs, check_vma=False)
```

```python
import jax
import jax.numpy as jnp
import ml_dtypes
import numpy as np
from jax import lax
from jax.experimental import pallas as pl
from jax.experimental.pallas import tpu as pltpu
from jax.sharding import PartitionSpec as P

C, NX, NY, NZ, NT = 20, 128, 128, 32, 24
KX, KY, KZ, KT = 24, 24, 16, 12
ZT, MZT = NZ * NT, KZ * KT
GX = GY = 16
RX, RY = NX // GX, NY // GY
BM = MZT // GX
H = BM * KX // GY
HQ = 2 * H
CM, CR = 16, 4
MAIN = BM * 2 * RX
ROWS = MAIN + BM * 2 * RX * CR // CM
LANES = 768
MIB = 1024 * 1024

NN = (((1,), (0,)), ((), ()))
NT_DIMS = (((1,), (1,)), ((), ()))


def slot_mode(slot):
    return (slot % 4) * 3 + slot // 4


def kept(count, length):
    steps = np.arange(count)
    return np.where(steps < count // 2, steps, length - count + steps)


def halves(table):
    table = table.astype(np.float32)
    high = table.astype(ml_dtypes.bfloat16)
    low = (table - high.astype(np.float32)).astype(ml_dtypes.bfloat16)
    return np.stack([high, low])


def depth_table():
    kz = kept(KZ, NZ)
    modes = np.array([g * BM + slot_mode(s) for g in range(GX) for s in range(BM)])
    z_freq, t_freq = kz[modes // KT], modes % KT
    cells = np.arange(ZT)
    turns = (z_freq[:, None] * (cells // NT)[None] * NT + t_freq[:, None] * (cells % NT)[None] * NZ) % ZT
    angle = turns * (2.0 * np.pi / ZT)
    cosine, sine = np.cos(angle), np.sin(angle)
    scale = (np.where(t_freq == 0, 1.0, 2.0) / (NX * NY * ZT))[:, None]
    inverse = np.stack([cosine * scale, -sine * scale], axis=1).reshape(2 * MZT, ZT)
    return stacked_table(inverse)


def x_tables():
    angle = (np.arange(NX)[:, None] * kept(KX, NX)[None] % NX) * (2.0 * np.pi / NX)
    cosine, sine = np.cos(angle), np.sin(angle)
    forward = np.stack([np.stack([cosine, -sine], -1), np.stack([sine, cosine], -1)], 1)
    back = np.stack([np.stack([cosine, -sine], -1), np.stack([sine, cosine], -1)], 1)
    shape = (GX, RX, 2, KX * 2)
    forward, back = forward.reshape(shape), back.reshape(shape)
    def main(table):
        return table.transpose(0, 2, 1, 3).reshape(GX * 2 * RX, KX * 2)
    def rest(table):
        return table.reshape(GX * RX * 2, KX * 2)
    return (
        np.stack([halves(main(forward).T), halves(rest(forward).T)]),
        np.stack([halves(main(back)), halves(rest(back))]),
    )


def y_tables():
    angle = (np.arange(NY)[:, None] * kept(KY, NY)[None] % NY) * (2.0 * np.pi / NY)
    cosine, sine = np.cos(angle), np.sin(angle)
    both = np.concatenate([cosine, sine], axis=1)
    return halves(both.T), halves(both)


def split(value):
    high = value.astype(jnp.bfloat16)
    return high, (value - high.astype(jnp.float32)).astype(jnp.bfloat16)


def product(left, right, dims):
    def term(a, b):
        return lax.dot_general(a, b, dims, preferred_element_type=jnp.float32)
    return term(left[0], right[0]) + (term(left[0], right[1]) + term(left[1], right[0]))


def stacked_left(value, axis):
    high, low = split(value)
    return jnp.concatenate([high, high, low], axis=axis)


def stacked_right(value, axis):
    high, low = split(value)
    return jnp.concatenate([high, low, high], axis=axis)


def stacked_table(table):
    high, low = halves(table)
    return np.concatenate([high, low, high], axis=0)


def dot(left, right, dims):
    return lax.dot_general(left, right, dims, preferred_element_type=jnp.float32)


def block_swap(value):
    row = lax.broadcasted_iota(jnp.int32, value.shape, 1) // 2
    lane = lax.broadcasted_iota(jnp.int32, value.shape, 2) // 32
    far = pltpu.roll(pltpu.roll(value, 4, 1), 64, 2)
    value = jnp.where((row // 2) == (lane // 2), value, far)
    up = pltpu.roll(pltpu.roll(value, 6, 1), 32, 2)
    down = pltpu.roll(pltpu.roll(value, 2, 1), 96, 2)
    return jnp.where((row % 2) == (lane % 2), value, jnp.where(row % 2 == 0, up, down))


def divide(value, by):
    return (value * 2731) >> 16 if by == 24 else value // by


def fill_forward_table(table):
    def cells(rows):
        row = lax.broadcasted_iota(jnp.int32, (rows, ZT), 0)
        lane = lax.broadcasted_iota(jnp.int32, (rows, ZT), 1)
        z = divide(lane, NT)
        return row, z, lane - NT * z
    row, z, _ = cells(GX)
    z_freq = jnp.where(row < KZ // 2, row, row + NZ - KZ)
    angle = ((z_freq * z) % NZ).astype(jnp.float32) * np.float32(2.0 * np.pi / NZ)
    z_cos, z_sin = jnp.cos(angle), jnp.sin(angle)
    row, _, t = cells(2 * BM)
    slot = row >> 1
    turns = ((slot & 3) * 3 + (slot >> 2)) * t
    angle = (turns - NT * divide(turns, NT)).astype(jnp.float32) * np.float32(2.0 * np.pi / NT)
    t_cos, t_sin = jnp.cos(angle), jnp.sin(angle)
    real = (row & 1) == 0
    one = jnp.where(real, t_cos, -t_sin)
    two = jnp.where(real, -t_sin, -t_cos)
    rows = [z_cos[g : g + 1] * one + z_sin[g : g + 1] * two for g in range(GX)]
    table[0], table[1] = split(jnp.concatenate(rows, axis=0))


def depth_kernel(field, out, held, held_table, arrived):
    copies = [
        pltpu.make_async_copy(field.at[:, pl.ds(2 * pair, 2)], held.at[pair], arrived.at[pair])
        for pair in range(4)
    ]
    for copy in copies:
        copy.start()
    fill_forward_table(held_table)
    tables = (held_table[0], held_table[1])
    for pair in range(4):
        if pair < 2:
            for copy in copies[pair : 1 + 3 * pair]:
                copy.wait()
        cells = jnp.concatenate(
            [held[pair, 0:CM, k].reshape(CM * RY, ZT) for k in range(2)], axis=0
        )
        modes = product(tables, split(cells), NT_DIMS)
        for k in range(2):
            for dest in range(GX):
                start = dest * ROWS + 2 * pair + k
                out[pl.ds(start, 2 * BM, stride=RX), :] = modes[
                    dest * 2 * BM : (dest + 1) * 2 * BM, k * 128 : (k + 1) * 128
                ]
    cells = jnp.concatenate(
        [held[k // 2, CM:C, k % 2].reshape(CR * RY, ZT) for k in range(RX)], axis=0
    )
    modes = product(tables, split(cells), NT_DIMS)
    for half in range(2):
        tiles = block_swap(modes[:, half * 128 : (half + 1) * 128].reshape(GX * 3, 8, 128))
        for dest in range(GX):
            for third in range(3):
                start = dest * ROWS + MAIN + third * 16 + half * 8
                out[pl.ds(start, 8), :] = tiles[dest * 3 + third]


def depth_transform(field):
    return pl.pallas_call(
        depth_kernel,
        in_specs=[pl.BlockSpec(memory_space=pltpu.HBM)],
        out_shape=jax.ShapeDtypeStruct((GX * ROWS, 128), jnp.float32),
        scratch_shapes=[
            pltpu.VMEM((4, C, 2, RY, ZT), jnp.float32),
            pltpu.VMEM((2, 2 * MZT, ZT), jnp.bfloat16),
            pltpu.SemaphoreType.DMA((4,)),
        ],
        compiler_params=pltpu.CompilerParams(vmem_limit_bytes=50 * MIB),
        cost_estimate=pl.CostEstimate(flops=2300000000, bytes_accessed=7000000, transcendentals=0),
        name="depth_forward",
    )(field)


def x_kernel(cells, table, out, held):
    main_table = (table[0, 0], table[0, 1])
    rest_table = (table[1, 0], table[1, 1])
    for slot in range(BM):
        columns = jnp.concatenate(
            [cells[pl.ds(s * ROWS + slot * 16, 16), :] for s in range(GX)], axis=0
        )
        mode = slot_mode(slot)
        held[pl.ds(mode * 2 * KX, 2 * KX), :] = product(main_table, split(columns), NN)
    for third in range(3):
        columns = jnp.concatenate(
            [cells[pl.ds(s * ROWS + MAIN + third * 16, 16), :] for s in range(GX)], axis=0
        )
        held[pl.ds((BM + third) * 2 * KX, 2 * KX), :] = product(rest_table, split(columns), NN)
    for g in range(GY):
        turned = held[pl.ds(g * HQ, HQ), :].T
        for c in range(CM):
            out[g, :, c * HQ : (c + 1) * HQ] = turned[c * RY : (c + 1) * RY]
    for b in range(4):
        turned = held[pl.ds(BM * 2 * KX + b * HQ, HQ), :].T
        for a in range(4):
            for c in range(CR):
                row = (a * CR + c) * RY
                out[4 * a + b, :, (CM + c) * HQ : (CM + c + 1) * HQ] = turned[row : row + RY]
    for g in range(GY):
        out[g, :, C * HQ : LANES] = jnp.zeros((RY, LANES - C * HQ), jnp.float32)


def x_transform(cells, table):
    return pl.pallas_call(
        x_kernel,
        out_shape=jax.ShapeDtypeStruct((GY, RY, LANES), jnp.float32),
        scratch_shapes=[pltpu.VMEM(((BM + 3) * 2 * KX, 128), jnp.float32)],
        compiler_params=pltpu.CompilerParams(vmem_limit_bytes=40 * MIB),
        cost_estimate=pl.CostEstimate(flops=150000000, bytes_accessed=2500000, transcendentals=0),
        name="x_forward",
    )(cells, table)


def even_lanes(shape):
    return lax.broadcasted_iota(jnp.int32, shape, len(shape) - 1) % 2 == 0


def turn_parts(value, even):
    lanes = value.shape[-1]
    return jnp.where(even, -pltpu.roll(value, lanes - 1, 1), pltpu.roll(value, 1, 1))


def mix_kernel(cells, weights, forward, back, out, reals, imags, mixed):
    sums = product((forward[0], forward[1]), split(cells[...].reshape(GY * RY, LANES)), NN)
    even = even_lanes((KY, LANES))
    coef = sums[:KY] - turn_parts(sums[KY:], even)
    real = jnp.where(even, coef, pltpu.roll(coef, 1, 1))
    imag = jnp.where(even, pltpu.roll(coef, LANES - 1, 1), coef)
    for i in range(C):
        reals[i] = real[:, i * HQ : (i + 1) * HQ]
        imags[i] = imag[:, i * HQ : (i + 1) * HQ]
    even_pairs = even_lanes((KY, HQ))
    group = 4
    for first in range(0, C, group):
        one = [jnp.zeros((KY, HQ), jnp.float32)] * group
        two = [jnp.zeros((KY, HQ), jnp.float32)] * group
        for i in range(C):
            real_i, imag_i = reals[i], imags[i]
            for k in range(group):
                weight = weights[i, first + k]
                one[k] = one[k] + weight * real_i
                two[k] = two[k] + weight * imag_i
        for k in range(group):
            o = first + k
            mixed[:, o * HQ : (o + 1) * HQ] = one[k] + turn_parts(two[k], even_pairs)
    mixed[:, C * HQ : LANES] = jnp.zeros((KY, LANES - C * HQ), jnp.float32)
    modes = mixed[...]
    both = jnp.concatenate([modes, turn_parts(modes, even)], axis=0)
    out[...] = product((back[0], back[1]), split(both), NN).reshape(GY, RY, LANES)


def mix_modes(cells, weights, forward, back):
    return pl.pallas_call(
        mix_kernel,
        out_shape=jax.ShapeDtypeStruct((GY, RY, LANES), jnp.float32),
        scratch_shapes=[
            pltpu.VMEM((C, KY, HQ), jnp.float32),
            pltpu.VMEM((C, KY, HQ), jnp.float32),
            pltpu.VMEM((KY, LANES), jnp.float32),
        ],
        compiler_params=pltpu.CompilerParams(vmem_limit_bytes=40 * MIB),
        cost_estimate=pl.CostEstimate(flops=60000000, bytes_accessed=6000000, transcendentals=0),
        name="y_mix",
    )(cells, weights, forward, back)


def x_back_kernel(modes, table, out, held):
    main_table = (table[0, 0], table[0, 1])
    rest_table = (table[1, 0], table[1, 1])
    for g in range(GY):
        rows = jnp.concatenate([modes[g, :, c * HQ : (c + 1) * HQ] for c in range(CM)], axis=0)
        held[pl.ds(g * HQ, HQ), :] = rows.T
    for b in range(4):
        rows = jnp.concatenate(
            [
                modes[4 * a + b, :, (CM + c) * HQ : (CM + c + 1) * HQ]
                for a in range(4)
                for c in range(CR)
            ],
            axis=0,
        )
        held[pl.ds(BM * 2 * KX + b * HQ, HQ), :] = rows.T
    for slot in range(BM):
        mode = slot_mode(slot)
        columns = held[pl.ds(mode * 2 * KX, 2 * KX), :]
        cells = product(main_table, split(columns), NN)
        for s in range(GX):
            out[pl.ds(s * ROWS + slot * 16, 16), :] = cells[s * 16 : (s + 1) * 16]
    for third in range(3):
        columns = held[pl.ds((BM + third) * 2 * KX, 2 * KX), :]
        cells = product(rest_table, split(columns), NN)
        for s in range(GX):
            out[pl.ds(s * ROWS + MAIN + third * 16, 16), :] = cells[s * 16 : (s + 1) * 16]


def x_back(modes, table):
    return pl.pallas_call(
        x_back_kernel,
        out_shape=jax.ShapeDtypeStruct((GX * ROWS, 128), jnp.float32),
        scratch_shapes=[pltpu.VMEM(((BM + 3) * 2 * KX, 128), jnp.float32)],
        compiler_params=pltpu.CompilerParams(vmem_limit_bytes=40 * MIB),
        cost_estimate=pl.CostEstimate(flops=150000000, bytes_accessed=2500000, transcendentals=0),
        name="x_back",
    )(modes, table)


def spread_map(channel_map):
    rows = C * RY
    copy = lax.broadcasted_iota(jnp.int32, (C, rows), 1) // RY
    copy = (copy == lax.broadcasted_iota(jnp.int32, (C, rows), 0)).astype(jnp.bfloat16)
    same = lax.broadcasted_iota(jnp.int32, (rows, rows), 0) % RY
    same = same == lax.broadcasted_iota(jnp.int32, (rows, rows), 1) % RY
    spread = []
    for half in split(channel_map):
        wide = lax.dot_general(half, copy, NN, preferred_element_type=jnp.float32)
        tall = jnp.broadcast_to(wide[:, None], (C, RY, rows)).reshape(rows, rows)
        spread.append(jnp.where(same, tall, 0.0).astype(jnp.bfloat16))
    return spread


def final_kernel(field, cells, table, channel_map, bias, out, rest, spread):
    step = pl.program_id(0)

    @pl.when(step == 0)
    def _():
        high, low = spread_map(channel_map[...])
        spread[...] = jnp.concatenate([high, high, low], axis=1)

    @pl.when(step % 2 == 0)
    def _():
        tiles = jnp.stack(
            [
                cells[pl.ds(pl.multiple_of(s * ROWS + MAIN + third * 16 + (step // 2) * 8, 8), 8), :]
                for s in range(GX)
                for third in range(3)
            ]
        )
        rest[...] = block_swap(tiles).reshape(2 * MZT, 128).T

    columns = []
    for k in range(2):
        main = jnp.concatenate(
            [cells[pl.ds(s * ROWS + 2 * step + k, 2 * BM, stride=RX), :] for s in range(GX)], axis=0
        ).T
        row = pl.multiple_of(((step % 2) * 2 + k) * CR * RY, CR * RY)
        columns += [main, rest[pl.ds(row, CR * RY), :]]
    spectral = dot(stacked_left(jnp.concatenate(columns, axis=0), 1), table[...], NN)
    for k in range(2):
        bypass = dot(spread[...], stacked_right(field[:, k].reshape(C * RY, ZT), 0), NN)
        value = spectral[k * C * RY : (k + 1) * C * RY] + bypass
        for c in range(C):
            one = value[c * RY : (c + 1) * RY] + bias[c]
            out[c, k] = 0.5 * one * (1.0 + lax.erf(one * np.float32(np.sqrt(0.5))))


def final_stage(field, cells, table, channel_map, bias):
    return pl.pallas_call(
        final_kernel,
        grid=(4,),
        in_specs=[
            pl.BlockSpec((C, 2, RY, ZT), lambda i: (0, i, 0, 0)),
            pl.BlockSpec((GX * ROWS, 128), lambda i: (0, 0)),
            pl.BlockSpec((3 * 2 * MZT, ZT), lambda i: (0, 0)),
            pl.BlockSpec((C, C), lambda i: (0, 0)),
            pl.BlockSpec(memory_space=pltpu.SMEM),
        ],
        out_specs=pl.BlockSpec((C, 2, RY, ZT), lambda i: (0, i, 0, 0)),
        out_shape=jax.ShapeDtypeStruct((C, RX, RY, ZT), jnp.float32),
        scratch_shapes=[
            pltpu.VMEM((128, 2 * MZT), jnp.float32),
            pltpu.VMEM((C * RY, 3 * C * RY), jnp.bfloat16),
        ],
        compiler_params=pltpu.CompilerParams(vmem_limit_bytes=40 * MIB),
        cost_estimate=pl.CostEstimate(flops=3200000000, bytes_accessed=11000000, transcendentals=1000000),
        name="depth_back",
    )(field, cells, table, channel_map, bias)


def exchange(value, axis):
    return lax.all_to_all(value, axis, split_axis=0, concat_axis=0, tiled=True)


def shards(field, spec_weight, bypass_weight, bypass_bias):
    x_forward, x_inverse = x_tables()
    y_forward, y_inverse = y_tables()
    field = field.reshape(C, RX, RY, ZT)
    modes = depth_transform(field)
    cells = exchange(modes.reshape(GX, ROWS, 128), "gx").reshape(GX * ROWS, 128)
    pairs = exchange(x_transform(cells, x_forward), "gy")
    mixed = exchange(mix_modes(pairs, spec_weight, y_forward, y_inverse), "gy")
    back = x_back(mixed, x_inverse)
    back = exchange(back.reshape(GX, ROWS, 128), "gx").reshape(GX * ROWS, 128)
    out = final_stage(field, back, depth_table(), bypass_weight, bypass_bias)
    return out.reshape(1, C, RX, RY, ZT)


def solution(mesh):
    in_specs = (P(None, None, "gx", "gy", None), P(None, None, None, ("gx", "gy")), P(), P())
    out_specs = P(None, None, "gx", "gy", None)
    return jax.shard_map(shards, mesh=mesh, in_specs=in_specs, out_specs=out_specs, check_vma=False)
```

```python
import jax
import jax.numpy as jnp
import ml_dtypes
import numpy as np
from jax import lax
from jax.experimental import pallas as pl
from jax.experimental.pallas import tpu as pltpu
from jax.sharding import PartitionSpec as P

C, NX, NY, NZ, NT = 20, 128, 128, 32, 24
KX, KY, KZ, KT = 24, 24, 16, 12
ZT, MZT = NZ * NT, KZ * KT
GX = GY = 16
RX, RY = NX // GX, NY // GY
BM = MZT // GX
H = BM * KX // GY
HQ = 2 * H
CM, CR = 16, 4
MAIN = BM * 2 * RX
ROWS = MAIN + BM * 2 * RX * CR // CM
LANES = 768
MIB = 1024 * 1024

NN = (((1,), (0,)), ((), ()))
NT_DIMS = (((1,), (1,)), ((), ()))


def slot_mode(slot):
    return (slot % 4) * 3 + slot // 4


def kept(count, length):
    steps = np.arange(count)
    return np.where(steps < count // 2, steps, length - count + steps)


def halves(table):
    table = table.astype(np.float32)
    high = table.astype(ml_dtypes.bfloat16)
    low = (table - high.astype(np.float32)).astype(ml_dtypes.bfloat16)
    return np.stack([high, low])


def depth_table():
    kz = kept(KZ, NZ)
    modes = np.array([g * BM + slot_mode(s) for g in range(GX) for s in range(BM)])
    z_freq, t_freq = kz[modes // KT], modes % KT
    cells = np.arange(ZT)
    turns = (z_freq[:, None] * (cells // NT)[None] * NT + t_freq[:, None] * (cells % NT)[None] * NZ) % ZT
    angle = turns * (2.0 * np.pi / ZT)
    cosine, sine = np.cos(angle), np.sin(angle)
    scale = (np.where(t_freq == 0, 1.0, 2.0) / (NX * NY * ZT))[:, None]
    inverse = np.stack([cosine * scale, -sine * scale], axis=1).reshape(2 * MZT, ZT)
    return stacked_table(inverse)


def x_tables():
    angle = (np.arange(NX)[:, None] * kept(KX, NX)[None] % NX) * (2.0 * np.pi / NX)
    cosine, sine = np.cos(angle), np.sin(angle)
    forward = np.stack([np.stack([cosine, -sine], -1), np.stack([sine, cosine], -1)], 1)
    back = np.stack([np.stack([cosine, -sine], -1), np.stack([sine, cosine], -1)], 1)
    shape = (GX, RX, 2, KX * 2)
    forward, back = forward.reshape(shape), back.reshape(shape)
    def main(table):
        return table.transpose(0, 2, 1, 3).reshape(GX * 2 * RX, KX * 2)
    def rest(table):
        return table.reshape(GX * RX * 2, KX * 2)
    return (
        np.stack([halves(main(forward).T), halves(rest(forward).T)]),
        np.stack([halves(main(back)), halves(rest(back))]),
    )


def y_tables():
    angle = (np.arange(NY)[:, None] * kept(KY, NY)[None] % NY) * (2.0 * np.pi / NY)
    cosine, sine = np.cos(angle), np.sin(angle)
    both = np.concatenate([cosine, sine], axis=1)
    return halves(both.T), halves(both)


def split(value):
    high = value.astype(jnp.bfloat16)
    return high, (value - high.astype(jnp.float32)).astype(jnp.bfloat16)


def product(left, right, dims):
    def term(a, b):
        return lax.dot_general(a, b, dims, preferred_element_type=jnp.float32)
    return term(left[0], right[0]) + (term(left[0], right[1]) + term(left[1], right[0]))


def stacked_left(value, axis):
    high, low = split(value)
    return jnp.concatenate([high, high, low], axis=axis)


def stacked_right(value, axis):
    high, low = split(value)
    return jnp.concatenate([high, low, high], axis=axis)


def stacked_table(table):
    high, low = halves(table)
    return np.concatenate([high, low, high], axis=0)


def dot(left, right, dims):
    return lax.dot_general(left, right, dims, preferred_element_type=jnp.float32)


def block_swap(value):
    row = lax.broadcasted_iota(jnp.int32, value.shape, 1) // 2
    lane = lax.broadcasted_iota(jnp.int32, value.shape, 2) // 32
    far = pltpu.roll(pltpu.roll(value, 4, 1), 64, 2)
    value = jnp.where((row // 2) == (lane // 2), value, far)
    up = pltpu.roll(pltpu.roll(value, 6, 1), 32, 2)
    down = pltpu.roll(pltpu.roll(value, 2, 1), 96, 2)
    return jnp.where((row % 2) == (lane % 2), value, jnp.where(row % 2 == 0, up, down))


def divide(value, by):
    return (value * 2731) >> 16 if by == 24 else value // by


def fill_forward_table(table):
    def cells(rows):
        row = lax.broadcasted_iota(jnp.int32, (rows, ZT), 0)
        lane = lax.broadcasted_iota(jnp.int32, (rows, ZT), 1)
        z = divide(lane, NT)
        return row, z, lane - NT * z
    row, z, _ = cells(GX)
    z_freq = jnp.where(row < KZ // 2, row, row + NZ - KZ)
    angle = ((z_freq * z) % NZ).astype(jnp.float32) * np.float32(2.0 * np.pi / NZ)
    z_cos, z_sin = jnp.cos(angle), jnp.sin(angle)
    row, _, t = cells(2 * BM)
    slot = row >> 1
    turns = ((slot & 3) * 3 + (slot >> 2)) * t
    angle = (turns - NT * divide(turns, NT)).astype(jnp.float32) * np.float32(2.0 * np.pi / NT)
    t_cos, t_sin = jnp.cos(angle), jnp.sin(angle)
    real = (row & 1) == 0
    one = jnp.where(real, t_cos, -t_sin)
    two = jnp.where(real, -t_sin, -t_cos)
    rows = [z_cos[g : g + 1] * one + z_sin[g : g + 1] * two for g in range(GX)]
    table[0], table[1] = split(jnp.concatenate(rows, axis=0))


def depth_kernel(field, out, held, held_table, arrived):
    copies = [
        pltpu.make_async_copy(field.at[:, pl.ds(2 * pair, 2)], held.at[pair], arrived.at[pair])
        for pair in range(4)
    ]
    for copy in copies:
        copy.start()
    fill_forward_table(held_table)
    tables = (held_table[0], held_table[1])
    for pair in range(4):
        if pair < 2:
            for copy in copies[pair : 1 + 3 * pair]:
                copy.wait()
        cells = jnp.concatenate(
            [held[pair, 0:CM, k].reshape(CM * RY, ZT) for k in range(2)], axis=0
        )
        modes = product(tables, split(cells), NT_DIMS)
        for k in range(2):
            for dest in range(GX):
                start = dest * ROWS + 2 * pair + k
                out[pl.ds(start, 2 * BM, stride=RX), :] = modes[
                    dest * 2 * BM : (dest + 1) * 2 * BM, k * 128 : (k + 1) * 128
                ]
    cells = jnp.concatenate(
        [held[k // 2, CM:C, k % 2].reshape(CR * RY, ZT) for k in range(RX)], axis=0
    )
    modes = product(tables, split(cells), NT_DIMS)
    for half in range(2):
        tiles = block_swap(modes[:, half * 128 : (half + 1) * 128].reshape(GX * 3, 8, 128))
        for dest in range(GX):
            for third in range(3):
                start = dest * ROWS + MAIN + third * 16 + half * 8
                out[pl.ds(start, 8), :] = tiles[dest * 3 + third]


def depth_transform(field):
    return pl.pallas_call(
        depth_kernel,
        in_specs=[pl.BlockSpec(memory_space=pltpu.HBM)],
        out_shape=jax.ShapeDtypeStruct((GX * ROWS, 128), jnp.float32),
        scratch_shapes=[
            pltpu.VMEM((4, C, 2, RY, ZT), jnp.float32),
            pltpu.VMEM((2, 2 * MZT, ZT), jnp.bfloat16),
            pltpu.SemaphoreType.DMA((4,)),
        ],
        compiler_params=pltpu.CompilerParams(vmem_limit_bytes=50 * MIB),
        cost_estimate=pl.CostEstimate(flops=2300000000, bytes_accessed=7000000, transcendentals=0),
        name="depth_forward",
    )(field)


def x_kernel(cells, table, out, held):
    main_table = (table[0, 0], table[0, 1])
    rest_table = (table[1, 0], table[1, 1])
    for slot in range(BM):
        columns = jnp.concatenate(
            [cells[pl.ds(s * ROWS + slot * 16, 16), :] for s in range(GX)], axis=0
        )
        mode = slot_mode(slot)
        held[pl.ds(mode * 2 * KX, 2 * KX), :] = product(main_table, split(columns), NN)
    for third in range(3):
        columns = jnp.concatenate(
            [cells[pl.ds(s * ROWS + MAIN + third * 16, 16), :] for s in range(GX)], axis=0
        )
        held[pl.ds((BM + third) * 2 * KX, 2 * KX), :] = product(rest_table, split(columns), NN)
    for g in range(GY):
        turned = held[pl.ds(g * HQ, HQ), :].T
        for c in range(CM):
            out[g, :, c * HQ : (c + 1) * HQ] = turned[c * RY : (c + 1) * RY]
    for b in range(4):
        turned = held[pl.ds(BM * 2 * KX + b * HQ, HQ), :].T
        for a in range(4):
            for c in range(CR):
                row = (a * CR + c) * RY
                out[4 * a + b, :, (CM + c) * HQ : (CM + c + 1) * HQ] = turned[row : row + RY]
    for g in range(GY):
        out[g, :, C * HQ : LANES] = jnp.zeros((RY, LANES - C * HQ), jnp.float32)


def x_transform(cells, table):
    return pl.pallas_call(
        x_kernel,
        out_shape=jax.ShapeDtypeStruct((GY, RY, LANES), jnp.float32),
        scratch_shapes=[pltpu.VMEM(((BM + 3) * 2 * KX, 128), jnp.float32)],
        compiler_params=pltpu.CompilerParams(vmem_limit_bytes=40 * MIB),
        cost_estimate=pl.CostEstimate(flops=150000000, bytes_accessed=2500000, transcendentals=0),
        name="x_forward",
    )(cells, table)


def even_lanes(shape):
    return lax.broadcasted_iota(jnp.int32, shape, len(shape) - 1) % 2 == 0


def turn_parts(value, even):
    lanes = value.shape[-1]
    return jnp.where(even, -pltpu.roll(value, lanes - 1, 1), pltpu.roll(value, 1, 1))


def mix_kernel(cells, weights, forward, back, out, reals, imags, mixed):
    sums = product((forward[0], forward[1]), split(cells[...].reshape(GY * RY, LANES)), NN)
    even = even_lanes((KY, LANES))
    coef = sums[:KY] - turn_parts(sums[KY:], even)
    real = jnp.where(even, coef, pltpu.roll(coef, 1, 1))
    imag = jnp.where(even, pltpu.roll(coef, LANES - 1, 1), coef)
    for i in range(C):
        reals[i] = real[:, i * HQ : (i + 1) * HQ]
        imags[i] = imag[:, i * HQ : (i + 1) * HQ]
    even_pairs = even_lanes((KY, HQ))
    group = 4
    for first in range(0, C, group):
        one = [jnp.zeros((KY, HQ), jnp.float32)] * group
        two = [jnp.zeros((KY, HQ), jnp.float32)] * group
        for i in range(C):
            real_i, imag_i = reals[i], imags[i]
            for k in range(group):
                weight = weights[i, first + k]
                one[k] = one[k] + weight * real_i
                two[k] = two[k] + weight * imag_i
        for k in range(group):
            o = first + k
            mixed[:, o * HQ : (o + 1) * HQ] = one[k] + turn_parts(two[k], even_pairs)
    mixed[:, C * HQ : LANES] = jnp.zeros((KY, LANES - C * HQ), jnp.float32)
    modes = mixed[...]
    both = jnp.concatenate([modes, turn_parts(modes, even)], axis=0)
    out[...] = product((back[0], back[1]), split(both), NN).reshape(GY, RY, LANES)


def mix_modes(cells, weights, forward, back):
    return pl.pallas_call(
        mix_kernel,
        out_shape=jax.ShapeDtypeStruct((GY, RY, LANES), jnp.float32),
        scratch_shapes=[
            pltpu.VMEM((C, KY, HQ), jnp.float32),
            pltpu.VMEM((C, KY, HQ), jnp.float32),
            pltpu.VMEM((KY, LANES), jnp.float32),
        ],
        compiler_params=pltpu.CompilerParams(vmem_limit_bytes=40 * MIB),
        cost_estimate=pl.CostEstimate(flops=60000000, bytes_accessed=6000000, transcendentals=0),
        name="y_mix",
    )(cells, weights, forward, back)


def x_back_kernel(modes, table, out, held):
    main_table = (table[0, 0], table[0, 1])
    rest_table = (table[1, 0], table[1, 1])
    for g in range(GY):
        rows = jnp.concatenate([modes[g, :, c * HQ : (c + 1) * HQ] for c in range(CM)], axis=0)
        held[pl.ds(g * HQ, HQ), :] = rows.T
    for b in range(4):
        rows = jnp.concatenate(
            [
                modes[4 * a + b, :, (CM + c) * HQ : (CM + c + 1) * HQ]
                for a in range(4)
                for c in range(CR)
            ],
            axis=0,
        )
        held[pl.ds(BM * 2 * KX + b * HQ, HQ), :] = rows.T
    for slot in range(BM):
        mode = slot_mode(slot)
        columns = held[pl.ds(mode * 2 * KX, 2 * KX), :]
        cells = product(main_table, split(columns), NN)
        for s in range(GX):
            out[pl.ds(s * ROWS + slot * 16, 16), :] = cells[s * 16 : (s + 1) * 16]
    for third in range(3):
        columns = held[pl.ds((BM + third) * 2 * KX, 2 * KX), :]
        cells = product(rest_table, split(columns), NN)
        for s in range(GX):
            out[pl.ds(s * ROWS + MAIN + third * 16, 16), :] = cells[s * 16 : (s + 1) * 16]


def x_back(modes, table):
    return pl.pallas_call(
        x_back_kernel,
        out_shape=jax.ShapeDtypeStruct((GX * ROWS, 128), jnp.float32),
        scratch_shapes=[pltpu.VMEM(((BM + 3) * 2 * KX, 128), jnp.float32)],
        compiler_params=pltpu.CompilerParams(vmem_limit_bytes=40 * MIB),
        cost_estimate=pl.CostEstimate(flops=150000000, bytes_accessed=2500000, transcendentals=0),
        name="x_back",
    )(modes, table)


def spread_map(channel_map):
    rows = C * RY
    copy = lax.broadcasted_iota(jnp.int32, (C, rows), 1) // RY
    copy = (copy == lax.broadcasted_iota(jnp.int32, (C, rows), 0)).astype(jnp.bfloat16)
    same = lax.broadcasted_iota(jnp.int32, (rows, rows), 0) % RY
    same = same == lax.broadcasted_iota(jnp.int32, (rows, rows), 1) % RY
    spread = []
    for half in split(channel_map):
        wide = lax.dot_general(half, copy, NN, preferred_element_type=jnp.float32)
        tall = jnp.broadcast_to(wide[:, None], (C, RY, rows)).reshape(rows, rows)
        spread.append(jnp.where(same, tall, 0.0).astype(jnp.bfloat16))
    return spread


def final_kernel(field, cells, table, channel_map, bias, out, held, left):
    high, low = spread_map(channel_map[...])
    spread = jnp.concatenate([high, high, low], axis=1)
    copies = []
    for pair in range(RX // 2):
        if pair % 2 == 0:
            tiles = jnp.stack(
                [
                    cells[pl.ds(s * ROWS + MAIN + third * 16 + (pair // 2) * 8, 8), :]
                    for s in range(GX)
                    for third in range(3)
                ]
            )
            rest = block_swap(tiles).reshape(2 * MZT, 128).T
        columns = []
        for k in range(2):
            main = jnp.concatenate(
                [cells[pl.ds(s * ROWS + 2 * pair + k, 2 * BM, stride=RX), :] for s in range(GX)],
                axis=0,
            )
            row = ((pair % 2) * 2 + k) * CR * RY
            columns += [main.T, rest[row : row + CR * RY]]
        spectral = dot(stacked_left(jnp.concatenate(columns, axis=0), 1), table[...], NN)
        for k in range(2):
            x = 2 * pair + k
            bypass = dot(spread, stacked_right(field[:, x].reshape(C * RY, ZT), 0), NN)
            value = spectral[k * C * RY : (k + 1) * C * RY] + bypass
            for c in range(C):
                one = value[c * RY : (c + 1) * RY] + bias[c]
                held[c, x] = 0.5 * one * (1.0 + lax.erf(one * np.float32(np.sqrt(0.5))))
            copies.append(pltpu.make_async_copy(held.at[:, x], out.at[:, x], left.at[x]))
            copies[-1].start()
    for copy in copies:
        copy.wait()


def final_stage(field, cells, table, channel_map, bias):
    whole = pl.BlockSpec(memory_space=pltpu.VMEM)
    return pl.pallas_call(
        final_kernel,
        in_specs=[whole, whole, whole, whole, pl.BlockSpec(memory_space=pltpu.SMEM)],
        out_specs=pl.BlockSpec(memory_space=pltpu.HBM),
        out_shape=jax.ShapeDtypeStruct((C, RX, RY, ZT), jnp.float32),
        scratch_shapes=[
            pltpu.VMEM((C, RX, RY, ZT), jnp.float32),
            pltpu.SemaphoreType.DMA((RX,)),
        ],
        compiler_params=pltpu.CompilerParams(vmem_limit_bytes=40 * MIB),
        cost_estimate=pl.CostEstimate(flops=3200000000, bytes_accessed=11000000, transcendentals=1000000),
        name="depth_back",
    )(field, cells, table, channel_map, bias)


def exchange(value, axis):
    return lax.all_to_all(value, axis, split_axis=0, concat_axis=0, tiled=True)


def shards(field, spec_weight, bypass_weight, bypass_bias):
    x_forward, x_inverse = x_tables()
    y_forward, y_inverse = y_tables()
    field = field.reshape(C, RX, RY, ZT)
    modes = depth_transform(field)
    cells = exchange(modes.reshape(GX, ROWS, 128), "gx").reshape(GX * ROWS, 128)
    pairs = exchange(x_transform(cells, x_forward), "gy")
    mixed = exchange(mix_modes(pairs, spec_weight, y_forward, y_inverse), "gy")
    back = x_back(mixed, x_inverse)
    back = exchange(back.reshape(GX, ROWS, 128), "gx").reshape(GX * ROWS, 128)
    out = final_stage(field, back, depth_table(), bypass_weight, bypass_bias)
    return out.reshape(1, C, RX, RY, ZT)


def solution(mesh):
    in_specs = (P(None, None, "gx", "gy", None), P(None, None, None, ("gx", "gy")), P(), P())
    out_specs = P(None, None, "gx", "gy", None)
    return jax.shard_map(shards, mesh=mesh, in_specs=in_specs, out_specs=out_specs, check_vma=False)
```

```python
import jax
import jax.numpy as jnp
import ml_dtypes
import numpy as np
from jax import lax
from jax.experimental import pallas as pl
from jax.experimental.pallas import tpu as pltpu
from jax.sharding import PartitionSpec as P

C, NX, NY, NZ, NT = 20, 128, 128, 32, 24
KX, KY, KZ, KT = 24, 24, 16, 12
ZT, MZT = NZ * NT, KZ * KT
GX = GY = 16
RX, RY = NX // GX, NY // GY
BM = MZT // GX
H = BM * KX // GY
HQ = 2 * H
CM, CR = 16, 4
MAIN = BM * 2 * RX
ROWS = MAIN + BM * 2 * RX * CR // CM
HALF = ZT // 2
LANES = 768
MIB = 1024 * 1024

NN = (((1,), (0,)), ((), ()))
NT_DIMS = (((1,), (1,)), ((), ()))


GY_ORDER = [x * 4 + z for z in range(4) for x in range(4)]


def slot_mode(slot):
    return (slot % 4) * 3 + slot // 4


def kept(count, length):
    steps = np.arange(count)
    return np.where(steps < count // 2, steps, length - count + steps)


def halves(table):
    table = table.astype(np.float32)
    high = table.astype(ml_dtypes.bfloat16)
    low = (table - high.astype(np.float32)).astype(ml_dtypes.bfloat16)
    return np.stack([high, low])


def depth_table():
    kz = kept(KZ, NZ)
    modes = np.array([g * BM + slot_mode(s) for g in range(GX) for s in range(BM)])
    z_freq, t_freq = kz[modes // KT], modes % KT
    cells = np.arange(ZT)
    turns = (z_freq[:, None] * (cells // NT)[None] * NT + t_freq[:, None] * (cells % NT)[None] * NZ) % ZT
    angle = turns * (2.0 * np.pi / ZT)
    cosine, sine = np.cos(angle), np.sin(angle)
    scale = (np.where(t_freq == 0, 1.0, 2.0) / (NX * NY * ZT))[:, None]
    inverse = np.stack([cosine * scale, -sine * scale], axis=1).reshape(2 * MZT, ZT)
    return stacked_table(inverse)


def x_tables():
    angle = (np.arange(NX)[:, None] * kept(KX, NX)[None] % NX) * (2.0 * np.pi / NX)
    cosine, sine = np.cos(angle), np.sin(angle)
    forward = np.stack([np.stack([cosine, -sine], -1), np.stack([sine, cosine], -1)], 1)
    back = np.stack([np.stack([cosine, -sine], -1), np.stack([sine, cosine], -1)], 1)
    shape = (GX, RX, 2, KX * 2)
    forward, back = forward.reshape(shape), back.reshape(shape)
    def main(table):
        return table.transpose(0, 2, 1, 3).reshape(GX * 2 * RX, KX * 2)
    def rest(table):
        return table.reshape(GX * RX * 2, KX * 2)
    return (
        np.stack([halves(main(forward).T), halves(rest(forward).T)]),
        np.stack([halves(main(back)), halves(rest(back))]),
    )


def y_tables():
    angle = (np.arange(NY)[:, None] * kept(KY, NY)[None] % NY) * (2.0 * np.pi / NY)
    cosine, sine = np.cos(angle), np.sin(angle)
    both = np.concatenate([cosine, sine], axis=1)
    both = both.reshape(GY, RY, 2 * KY)[np.array(GY_ORDER)].reshape(NY, 2 * KY)
    return halves(both.T), halves(both)


def split(value):
    high = value.astype(jnp.bfloat16)
    return high, (value - high.astype(jnp.float32)).astype(jnp.bfloat16)


def product(left, right, dims):
    def term(a, b):
        return lax.dot_general(a, b, dims, preferred_element_type=jnp.float32)
    return term(left[0], right[0]) + (term(left[0], right[1]) + term(left[1], right[0]))


def stacked_left(value, axis):
    high, low = split(value)
    return jnp.concatenate([high, high, low], axis=axis)


def stacked_right(value, axis):
    high, low = split(value)
    return jnp.concatenate([high, low, high], axis=axis)


def stacked_table(table):
    high, low = halves(table)
    return np.concatenate([high, low, high], axis=0)


def dot(left, right, dims):
    return lax.dot_general(left, right, dims, preferred_element_type=jnp.float32)


def block_swap(value):
    row = lax.broadcasted_iota(jnp.int32, value.shape, 1) // 2
    lane = lax.broadcasted_iota(jnp.int32, value.shape, 2) // 32
    far = pltpu.roll(pltpu.roll(value, 4, 1), 64, 2)
    value = jnp.where((row // 2) == (lane // 2), value, far)
    up = pltpu.roll(pltpu.roll(value, 6, 1), 32, 2)
    down = pltpu.roll(pltpu.roll(value, 2, 1), 96, 2)
    return jnp.where((row % 2) == (lane % 2), value, jnp.where(row % 2 == 0, up, down))


def divide(value, by):
    return (value * 2731) >> 16 if by == 24 else value // by


def fill_forward_table(table):
    def cells(rows):
        row = lax.broadcasted_iota(jnp.int32, (rows, HALF), 0)
        lane = lax.broadcasted_iota(jnp.int32, (rows, HALF), 1)
        z = divide(lane, NT)
        return row, z, lane - NT * z
    row, z, _ = cells(GX)
    z_freq = jnp.where(row < KZ // 2, row, row + NZ - KZ)
    angle = ((z_freq * z) % NZ).astype(jnp.float32) * np.float32(2.0 * np.pi / NZ)
    z_cos, z_sin = jnp.cos(angle), jnp.sin(angle)
    row, _, t = cells(2 * BM)
    slot = row >> 1
    turns = ((slot & 3) * 3 + (slot >> 2)) * t
    angle = (turns - NT * divide(turns, NT)).astype(jnp.float32) * np.float32(2.0 * np.pi / NT)
    t_cos, t_sin = jnp.cos(angle), jnp.sin(angle)
    real = (row & 1) == 0
    one = jnp.where(real, t_cos, -t_sin)
    two = jnp.where(real, -t_sin, -t_cos)
    for odd in range(2):
        rows = [z_cos[g : g + 1] * one + z_sin[g : g + 1] * two for g in range(odd, GX, 2)]
        table[odd] = stacked_left(jnp.concatenate(rows, axis=0), 1)


def depth_modes(cells, table):
    near, far = cells[:, :HALF], cells[:, HALF:]
    return [
        dot(table[odd], stacked_right(near - far if odd else near + far, 1), NT_DIMS)
        for odd in range(2)
    ]


def depth_kernel(field, out, held, table, arrived):
    copies = [
        pltpu.make_async_copy(field.at[:, pl.ds(2 * pair, 2)], held.at[pair], arrived.at[pair])
        for pair in range(4)
    ]
    for copy in copies:
        copy.start()
    fill_forward_table(table)
    for pair in range(4):
        if pair < 2:
            for copy in copies[pair : 1 + 3 * pair]:
                copy.wait()
        cells = jnp.concatenate(
            [held[pair, 0:CM, k].reshape(CM * RY, ZT) for k in range(2)], axis=0
        )
        modes = depth_modes(cells, table)
        for k in range(2):
            for dest in range(GX):
                start = dest * ROWS + 2 * pair + k
                row = dest // 2 * 2 * BM
                out[pl.ds(start, 2 * BM, stride=RX), :] = modes[dest % 2][
                    row : row + 2 * BM, k * 128 : (k + 1) * 128
                ]
    cells = jnp.concatenate(
        [held[k // 2, CM:C, k % 2].reshape(CR * RY, ZT) for k in range(RX)], axis=0
    )
    modes = depth_modes(cells, table)
    for half in range(2):
        for odd in range(2):
            tiles = block_swap(modes[odd][:, half * 128 : (half + 1) * 128].reshape(GX // 2 * 3, 8, 128))
            for dest in range(odd, GX, 2):
                for third in range(3):
                    start = dest * ROWS + MAIN + third * 16 + half * 8
                    out[pl.ds(start, 8), :] = tiles[dest // 2 * 3 + third]


def depth_transform(field):
    return pl.pallas_call(
        depth_kernel,
        in_specs=[pl.BlockSpec(memory_space=pltpu.HBM)],
        out_shape=jax.ShapeDtypeStruct((GX * ROWS, 128), jnp.float32),
        scratch_shapes=[
            pltpu.VMEM((4, C, 2, RY, ZT), jnp.float32),
            pltpu.VMEM((2, MZT, 3 * HALF), jnp.bfloat16),
            pltpu.SemaphoreType.DMA((4,)),
        ],
        compiler_params=pltpu.CompilerParams(vmem_limit_bytes=50 * MIB),
        cost_estimate=pl.CostEstimate(flops=1200000000, bytes_accessed=6000000, transcendentals=0),
        name="depth_forward",
    )(field)


def x_kernel(cells, table, out, held):
    main_table = (table[0, 0], table[0, 1])
    rest_table = (table[1, 0], table[1, 1])
    for slot in range(BM):
        columns = jnp.concatenate(
            [cells[pl.ds(s * ROWS + slot * 16, 16), :] for s in range(GX)], axis=0
        )
        mode = slot_mode(slot)
        held[pl.ds(mode * 2 * KX, 2 * KX), :] = product(main_table, split(columns), NN)
    for third in range(3):
        columns = jnp.concatenate(
            [cells[pl.ds(s * ROWS + MAIN + third * 16, 16), :] for s in range(GX)], axis=0
        )
        held[pl.ds((BM + third) * 2 * KX, 2 * KX), :] = product(rest_table, split(columns), NN)
    for g in range(GY):
        place = GY_ORDER.index(g)
        turned = held[pl.ds(g * HQ, HQ), :].T
        for c in range(CM):
            out[place, :, c * HQ : (c + 1) * HQ] = turned[c * RY : (c + 1) * RY]
    for b in range(4):
        turned = held[pl.ds(BM * 2 * KX + b * HQ, HQ), :].T
        for a in range(4):
            for c in range(CR):
                row = (a * CR + c) * RY
                out[GY_ORDER.index(4 * a + b), :, (CM + c) * HQ : (CM + c + 1) * HQ] = turned[row : row + RY]
    for g in range(GY):
        out[g, :, C * HQ : LANES] = jnp.zeros((RY, LANES - C * HQ), jnp.float32)


def x_transform(cells, table):
    return pl.pallas_call(
        x_kernel,
        out_shape=jax.ShapeDtypeStruct((GY, RY, LANES), jnp.float32),
        scratch_shapes=[pltpu.VMEM(((BM + 3) * 2 * KX, 128), jnp.float32)],
        compiler_params=pltpu.CompilerParams(vmem_limit_bytes=40 * MIB),
        cost_estimate=pl.CostEstimate(flops=150000000, bytes_accessed=2500000, transcendentals=0),
        name="x_forward",
    )(cells, table)


def even_lanes(shape):
    return lax.broadcasted_iota(jnp.int32, shape, len(shape) - 1) % 2 == 0


def turn_parts(value, even):
    lanes = value.shape[-1]
    return jnp.where(even, -pltpu.roll(value, lanes - 1, 1), pltpu.roll(value, 1, 1))


def mix_kernel(cells, weights, forward, back, out, reals, imags, mixed):
    sums = product((forward[0], forward[1]), split(cells[...].reshape(GY * RY, LANES)), NN)
    even = even_lanes((KY, LANES))
    coef = sums[:KY] - turn_parts(sums[KY:], even)
    real = jnp.where(even, coef, pltpu.roll(coef, 1, 1))
    imag = jnp.where(even, pltpu.roll(coef, LANES - 1, 1), coef)
    for i in range(C):
        reals[i] = real[:, i * HQ : (i + 1) * HQ]
        imags[i] = imag[:, i * HQ : (i + 1) * HQ]
    even_pairs = even_lanes((KY, HQ))
    group = 4
    for first in range(0, C, group):
        one = [jnp.zeros((KY, HQ), jnp.float32)] * group
        two = [jnp.zeros((KY, HQ), jnp.float32)] * group
        for i in range(C):
            real_i, imag_i = reals[i], imags[i]
            for k in range(group):
                weight = weights[i, first + k]
                one[k] = one[k] + weight * real_i
                two[k] = two[k] + weight * imag_i
        for k in range(group):
            o = first + k
            mixed[:, o * HQ : (o + 1) * HQ] = one[k] + turn_parts(two[k], even_pairs)
    mixed[:, C * HQ : LANES] = jnp.zeros((KY, LANES - C * HQ), jnp.float32)
    modes = mixed[...]
    both = jnp.concatenate([modes, turn_parts(modes, even)], axis=0)
    out[...] = product((back[0], back[1]), split(both), NN).reshape(GY, RY, LANES)


def mix_modes(cells, weights, forward, back):
    return pl.pallas_call(
        mix_kernel,
        out_shape=jax.ShapeDtypeStruct((GY, RY, LANES), jnp.float32),
        scratch_shapes=[
            pltpu.VMEM((C, KY, HQ), jnp.float32),
            pltpu.VMEM((C, KY, HQ), jnp.float32),
            pltpu.VMEM((KY, LANES), jnp.float32),
        ],
        compiler_params=pltpu.CompilerParams(vmem_limit_bytes=40 * MIB),
        cost_estimate=pl.CostEstimate(flops=60000000, bytes_accessed=6000000, transcendentals=0),
        name="y_mix",
    )(cells, weights, forward, back)


def x_back_kernel(modes, table, out, held):
    main_table = (table[0, 0], table[0, 1])
    rest_table = (table[1, 0], table[1, 1])
    for g in range(GY):
        place = GY_ORDER.index(g)
        rows = jnp.concatenate([modes[place, :, c * HQ : (c + 1) * HQ] for c in range(CM)], axis=0)
        held[pl.ds(g * HQ, HQ), :] = rows.T
    for b in range(4):
        rows = jnp.concatenate(
            [
                modes[GY_ORDER.index(4 * a + b), :, (CM + c) * HQ : (CM + c + 1) * HQ]
                for a in range(4)
                for c in range(CR)
            ],
            axis=0,
        )
        held[pl.ds(BM * 2 * KX + b * HQ, HQ), :] = rows.T
    for slot in range(BM):
        mode = slot_mode(slot)
        columns = held[pl.ds(mode * 2 * KX, 2 * KX), :]
        cells = product(main_table, split(columns), NN)
        for s in range(GX):
            out[pl.ds(s * ROWS + slot * 16, 16), :] = cells[s * 16 : (s + 1) * 16]
    for third in range(3):
        columns = held[pl.ds((BM + third) * 2 * KX, 2 * KX), :]
        cells = product(rest_table, split(columns), NN)
        for s in range(GX):
            out[pl.ds(s * ROWS + MAIN + third * 16, 16), :] = cells[s * 16 : (s + 1) * 16]


def x_back(modes, table):
    return pl.pallas_call(
        x_back_kernel,
        out_shape=jax.ShapeDtypeStruct((GX * ROWS, 128), jnp.float32),
        scratch_shapes=[pltpu.VMEM(((BM + 3) * 2 * KX, 128), jnp.float32)],
        compiler_params=pltpu.CompilerParams(vmem_limit_bytes=40 * MIB),
        cost_estimate=pl.CostEstimate(flops=150000000, bytes_accessed=2500000, transcendentals=0),
        name="x_back",
    )(modes, table)


def spread_map(channel_map):
    rows = C * RY
    copy = lax.broadcasted_iota(jnp.int32, (C, rows), 1) // RY
    copy = (copy == lax.broadcasted_iota(jnp.int32, (C, rows), 0)).astype(jnp.bfloat16)
    same = lax.broadcasted_iota(jnp.int32, (rows, rows), 0) % RY
    same = same == lax.broadcasted_iota(jnp.int32, (rows, rows), 1) % RY
    spread = []
    for half in split(channel_map):
        wide = lax.dot_general(half, copy, NN, preferred_element_type=jnp.float32)
        tall = jnp.broadcast_to(wide[:, None], (C, RY, rows)).reshape(rows, rows)
        spread.append(jnp.where(same, tall, 0.0).astype(jnp.bfloat16))
    return spread


def final_kernel(field, cells, table, channel_map, bias, out, held, left):
    high, low = spread_map(channel_map[...])
    spread = jnp.concatenate([high, high, low], axis=1)
    copies = []
    for pair in range(RX // 2):
        if pair % 2 == 0:
            tiles = jnp.stack(
                [
                    cells[pl.ds(s * ROWS + MAIN + third * 16 + (pair // 2) * 8, 8), :]
                    for s in range(GX)
                    for third in range(3)
                ]
            )
            rest = block_swap(tiles).reshape(2 * MZT, 128).T
        columns = []
        for k in range(2):
            main = jnp.concatenate(
                [cells[pl.ds(s * ROWS + 2 * pair + k, 2 * BM, stride=RX), :] for s in range(GX)],
                axis=0,
            )
            row = ((pair % 2) * 2 + k) * CR * RY
            columns += [main.T, rest[row : row + CR * RY]]
        spectral = dot(stacked_left(jnp.concatenate(columns, axis=0), 1), table[...], NN)
        for k in range(2):
            x = 2 * pair + k
            bypass = dot(spread, stacked_right(field[:, x].reshape(C * RY, ZT), 0), NN)
            value = spectral[k * C * RY : (k + 1) * C * RY] + bypass
            for c in range(C):
                one = value[c * RY : (c + 1) * RY] + bias[c]
                held[c, x] = 0.5 * one * (1.0 + lax.erf(one * np.float32(np.sqrt(0.5))))
            copies.append(pltpu.make_async_copy(held.at[:, x], out.at[:, x], left.at[x]))
            copies[-1].start()
    for copy in copies:
        copy.wait()


def final_stage(field, cells, table, channel_map, bias):
    whole = pl.BlockSpec(memory_space=pltpu.VMEM)
    return pl.pallas_call(
        final_kernel,
        in_specs=[whole, whole, whole, whole, pl.BlockSpec(memory_space=pltpu.SMEM)],
        out_specs=pl.BlockSpec(memory_space=pltpu.HBM),
        out_shape=jax.ShapeDtypeStruct((C, RX, RY, ZT), jnp.float32),
        scratch_shapes=[
            pltpu.VMEM((C, RX, RY, ZT), jnp.float32),
            pltpu.SemaphoreType.DMA((RX,)),
        ],
        compiler_params=pltpu.CompilerParams(vmem_limit_bytes=40 * MIB),
        cost_estimate=pl.CostEstimate(flops=3200000000, bytes_accessed=11000000, transcendentals=1000000),
        name="depth_back",
    )(field, cells, table, channel_map, bias)


def exchange(value, axis, groups=None):
    return lax.all_to_all(
        value, axis, split_axis=0, concat_axis=0, axis_index_groups=groups, tiled=True
    )


def shards(field, spec_weight, bypass_weight, bypass_bias):
    x_forward, x_inverse = x_tables()
    y_forward, y_inverse = y_tables()
    field = field.reshape(C, RX, RY, ZT)
    modes = depth_transform(field)
    cells = exchange(modes.reshape(GX, ROWS, 128), "gx").reshape(GX * ROWS, 128)
    pairs = exchange(x_transform(cells, x_forward), "gy", [GY_ORDER])
    mixed = exchange(mix_modes(pairs, spec_weight, y_forward, y_inverse), "gy", [GY_ORDER])
    back = x_back(mixed, x_inverse)
    back = exchange(back.reshape(GX, ROWS, 128), "gx").reshape(GX * ROWS, 128)
    out = final_stage(field, back, depth_table(), bypass_weight, bypass_bias)
    return out.reshape(1, C, RX, RY, ZT)


def solution(mesh):
    in_specs = (P(None, None, "gx", "gy", None), P(None, None, None, ("gx", "gy")), P(), P())
    out_specs = P(None, None, "gx", "gy", None)
    return jax.shard_map(shards, mesh=mesh, in_specs=in_specs, out_specs=out_specs, check_vma=False)
```

```python
import jax
import jax.numpy as jnp
import ml_dtypes
import numpy as np
from jax import lax
from jax.experimental import pallas as pl
from jax.experimental.pallas import tpu as pltpu
from jax.sharding import PartitionSpec as P

C, NX, NY, NZ, NT = 20, 128, 128, 32, 24
KX, KY, KZ, KT = 24, 24, 16, 12
ZT, MZT = NZ * NT, KZ * KT
GX = GY = 16
RX, RY = NX // GX, NY // GY
BM = MZT // GX
H = BM * KX // GY
HQ = 2 * H
CM, CR = 16, 4
MAIN = BM * 2 * RX
ROWS = MAIN + BM * 2 * RX * CR // CM
HALF = ZT // 2
LANES = 768
MIB = 1024 * 1024

NN = (((1,), (0,)), ((), ()))
NT_DIMS = (((1,), (1,)), ((), ()))


GY_ORDER = [x * 4 + z for z in range(4) for x in range(4)]


def slot_mode(slot):
    return (slot % 4) * 3 + slot // 4


def kept(count, length):
    steps = np.arange(count)
    return np.where(steps < count // 2, steps, length - count + steps)


def halves(table):
    table = table.astype(np.float32)
    high = table.astype(ml_dtypes.bfloat16)
    low = (table - high.astype(np.float32)).astype(ml_dtypes.bfloat16)
    return np.stack([high, low])


def depth_table():
    kz = kept(KZ, NZ)
    modes = np.array([g * BM + slot_mode(s) for g in range(GX) for s in range(BM)])
    z_freq, t_freq = kz[modes // KT], modes % KT
    cells = np.arange(ZT)
    turns = (z_freq[:, None] * (cells // NT)[None] * NT + t_freq[:, None] * (cells % NT)[None] * NZ) % ZT
    angle = turns * (2.0 * np.pi / ZT)
    cosine, sine = np.cos(angle), np.sin(angle)
    scale = (np.where(t_freq == 0, 1.0, 2.0) / (NX * NY * ZT))[:, None]
    inverse = np.stack([cosine * scale, -sine * scale], axis=1).reshape(2 * MZT, ZT)
    return right_table(inverse)


def x_tables():
    angle = (np.arange(NX)[:, None] * kept(KX, NX)[None] % NX) * (2.0 * np.pi / NX)
    cosine, sine = np.cos(angle), np.sin(angle)
    forward = np.stack([np.stack([cosine, -sine], -1), np.stack([sine, cosine], -1)], 1)
    back = np.stack([np.stack([cosine, -sine], -1), np.stack([sine, cosine], -1)], 1)
    shape = (GX, RX, 2, KX * 2)
    forward, back = forward.reshape(shape), back.reshape(shape)
    def main(table):
        return table.transpose(0, 2, 1, 3).reshape(GX * 2 * RX, KX * 2)
    def rest(table):
        return table.reshape(GX * RX * 2, KX * 2)
    return (
        np.stack([left_table(main(forward).T), left_table(rest(forward).T)]),
        np.stack([left_table(main(back)), left_table(rest(back))]),
    )


def y_tables():
    angle = (np.arange(NY)[:, None] * kept(KY, NY)[None] % NY) * (2.0 * np.pi / NY)
    cosine, sine = np.cos(angle), np.sin(angle)
    both = np.concatenate([cosine, sine], axis=1)
    both = both.reshape(GY, RY, 2 * KY)[np.array(GY_ORDER)].reshape(NY, 2 * KY)
    return left_table(both.T), left_table(both)


def split(value):
    high = value.astype(jnp.bfloat16)
    return high, (value - high.astype(jnp.float32)).astype(jnp.bfloat16)


def stacked_left(value, axis):
    high, low = split(value)
    return jnp.concatenate([high, high, low], axis=axis)


def stacked_right(value, axis):
    high, low = split(value)
    return jnp.concatenate([high, low, high], axis=axis)


def left_table(table):
    high, low = halves(table)
    return np.concatenate([high, high, low], axis=1)


def right_table(table):
    high, low = halves(table)
    return np.concatenate([high, low, high], axis=0)


def dot(left, right, dims):
    return lax.dot_general(left, right, dims, preferred_element_type=jnp.float32)


def block_swap(value):
    row = lax.broadcasted_iota(jnp.int32, value.shape, 1) // 2
    lane = lax.broadcasted_iota(jnp.int32, value.shape, 2) // 32
    far = pltpu.roll(pltpu.roll(value, 4, 1), 64, 2)
    value = jnp.where((row // 2) == (lane // 2), value, far)
    up = pltpu.roll(pltpu.roll(value, 6, 1), 32, 2)
    down = pltpu.roll(pltpu.roll(value, 2, 1), 96, 2)
    return jnp.where((row % 2) == (lane % 2), value, jnp.where(row % 2 == 0, up, down))


def divide(value, by):
    return (value * 2731) >> 16 if by == 24 else value // by


def fill_forward_table(table):
    def cells(rows):
        row = lax.broadcasted_iota(jnp.int32, (rows, HALF), 0)
        lane = lax.broadcasted_iota(jnp.int32, (rows, HALF), 1)
        z = divide(lane, NT)
        return row, z, lane - NT * z
    row, z, _ = cells(GX)
    z_freq = jnp.where(row < KZ // 2, row, row + NZ - KZ)
    angle = ((z_freq * z) % NZ).astype(jnp.float32) * np.float32(2.0 * np.pi / NZ)
    z_cos, z_sin = jnp.cos(angle), jnp.sin(angle)
    row, _, t = cells(2 * BM)
    slot = row >> 1
    turns = ((slot & 3) * 3 + (slot >> 2)) * t
    angle = (turns - NT * divide(turns, NT)).astype(jnp.float32) * np.float32(2.0 * np.pi / NT)
    t_cos, t_sin = jnp.cos(angle), jnp.sin(angle)
    real = (row & 1) == 0
    one = jnp.where(real, t_cos, -t_sin)
    two = jnp.where(real, -t_sin, -t_cos)
    for odd in range(2):
        rows = [z_cos[g : g + 1] * one + z_sin[g : g + 1] * two for g in range(odd, GX, 2)]
        table[odd] = stacked_left(jnp.concatenate(rows, axis=0), 1)


def depth_modes(cells, table):
    near, far = cells[:, :HALF], cells[:, HALF:]
    return [
        dot(table[odd], stacked_right(near - far if odd else near + far, 1), NT_DIMS)
        for odd in range(2)
    ]


def depth_kernel(field, out, held, table, arrived):
    copies = [
        pltpu.make_async_copy(field.at[:, pl.ds(2 * pair, 2)], held.at[pair], arrived.at[pair])
        for pair in range(4)
    ]
    for copy in copies:
        copy.start()
    fill_forward_table(table)
    for pair in range(4):
        if pair < 2:
            for copy in copies[pair : 1 + 3 * pair]:
                copy.wait()
        cells = jnp.concatenate(
            [held[pair, 0:CM, k].reshape(CM * RY, ZT) for k in range(2)], axis=0
        )
        modes = depth_modes(cells, table)
        for k in range(2):
            for dest in range(GX):
                start = dest * ROWS + 2 * pair + k
                row = dest // 2 * 2 * BM
                out[pl.ds(start, 2 * BM, stride=RX), :] = modes[dest % 2][
                    row : row + 2 * BM, k * 128 : (k + 1) * 128
                ]
    cells = jnp.concatenate(
        [held[k // 2, CM:C, k % 2].reshape(CR * RY, ZT) for k in range(RX)], axis=0
    )
    modes = depth_modes(cells, table)
    for half in range(2):
        for odd in range(2):
            tiles = block_swap(modes[odd][:, half * 128 : (half + 1) * 128].reshape(GX // 2 * 3, 8, 128))
            for dest in range(odd, GX, 2):
                for third in range(3):
                    start = dest * ROWS + MAIN + third * 16 + half * 8
                    out[pl.ds(start, 8), :] = tiles[dest // 2 * 3 + third]


def depth_transform(field):
    return pl.pallas_call(
        depth_kernel,
        in_specs=[pl.BlockSpec(memory_space=pltpu.HBM)],
        out_shape=jax.ShapeDtypeStruct((GX * ROWS, 128), jnp.float32),
        scratch_shapes=[
            pltpu.VMEM((4, C, 2, RY, ZT), jnp.float32),
            pltpu.VMEM((2, MZT, 3 * HALF), jnp.bfloat16),
            pltpu.SemaphoreType.DMA((4,)),
        ],
        compiler_params=pltpu.CompilerParams(vmem_limit_bytes=50 * MIB),
        cost_estimate=pl.CostEstimate(flops=1200000000, bytes_accessed=6000000, transcendentals=0),
        name="depth_forward",
    )(field)


def x_kernel(cells, table, out, held):
    main_table, rest_table = table[0], table[1]
    for slot in range(BM):
        columns = jnp.concatenate(
            [cells[pl.ds(s * ROWS + slot * 16, 16), :] for s in range(GX)], axis=0
        )
        mode = slot_mode(slot)
        held[pl.ds(mode * 2 * KX, 2 * KX), :] = dot(main_table, stacked_right(columns, 0), NN)
    for third in range(3):
        columns = jnp.concatenate(
            [cells[pl.ds(s * ROWS + MAIN + third * 16, 16), :] for s in range(GX)], axis=0
        )
        held[pl.ds((BM + third) * 2 * KX, 2 * KX), :] = dot(rest_table, stacked_right(columns, 0), NN)
    for g in range(GY):
        place = GY_ORDER.index(g)
        turned = held[pl.ds(g * HQ, HQ), :].T
        for c in range(CM):
            out[place, :, c * HQ : (c + 1) * HQ] = turned[c * RY : (c + 1) * RY]
    for b in range(4):
        turned = held[pl.ds(BM * 2 * KX + b * HQ, HQ), :].T
        for a in range(4):
            for c in range(CR):
                row = (a * CR + c) * RY
                out[GY_ORDER.index(4 * a + b), :, (CM + c) * HQ : (CM + c + 1) * HQ] = turned[row : row + RY]
    for g in range(GY):
        out[g, :, C * HQ : LANES] = jnp.zeros((RY, LANES - C * HQ), jnp.float32)


def x_transform(cells, table):
    return pl.pallas_call(
        x_kernel,
        out_shape=jax.ShapeDtypeStruct((GY, RY, LANES), jnp.float32),
        scratch_shapes=[pltpu.VMEM(((BM + 3) * 2 * KX, 128), jnp.float32)],
        compiler_params=pltpu.CompilerParams(vmem_limit_bytes=40 * MIB),
        cost_estimate=pl.CostEstimate(flops=150000000, bytes_accessed=2500000, transcendentals=0),
        name="x_forward",
    )(cells, table)


def even_lanes(shape):
    return lax.broadcasted_iota(jnp.int32, shape, len(shape) - 1) % 2 == 0


def turn_parts(value, even):
    lanes = value.shape[-1]
    return jnp.where(even, -pltpu.roll(value, lanes - 1, 1), pltpu.roll(value, 1, 1))


def mix_kernel(cells, weights, forward, back, out, reals, imags, mixed):
    sums = dot(forward[...], stacked_right(cells[...].reshape(GY * RY, LANES), 0), NN)
    even = even_lanes((KY, LANES))
    coef = sums[:KY] - turn_parts(sums[KY:], even)
    real = jnp.where(even, coef, pltpu.roll(coef, 1, 1))
    imag = jnp.where(even, pltpu.roll(coef, LANES - 1, 1), coef)
    for i in range(C):
        reals[i] = real[:, i * HQ : (i + 1) * HQ]
        imags[i] = imag[:, i * HQ : (i + 1) * HQ]
    even_pairs = even_lanes((KY, HQ))
    group = 4
    for first in range(0, C, group):
        one = [jnp.zeros((KY, HQ), jnp.float32)] * group
        two = [jnp.zeros((KY, HQ), jnp.float32)] * group
        for i in range(C):
            real_i, imag_i = reals[i], imags[i]
            for k in range(group):
                weight = weights[i, first + k]
                one[k] = one[k] + weight * real_i
                two[k] = two[k] + weight * imag_i
        for k in range(group):
            o = first + k
            mixed[:, o * HQ : (o + 1) * HQ] = one[k] + turn_parts(two[k], even_pairs)
    mixed[:, C * HQ : LANES] = jnp.zeros((KY, LANES - C * HQ), jnp.float32)
    modes = mixed[...]
    both = jnp.concatenate([modes, turn_parts(modes, even)], axis=0)
    out[...] = dot(back[...], stacked_right(both, 0), NN).reshape(GY, RY, LANES)


def mix_modes(cells, weights, forward, back):
    return pl.pallas_call(
        mix_kernel,
        out_shape=jax.ShapeDtypeStruct((GY, RY, LANES), jnp.float32),
        scratch_shapes=[
            pltpu.VMEM((C, KY, HQ), jnp.float32),
            pltpu.VMEM((C, KY, HQ), jnp.float32),
            pltpu.VMEM((KY, LANES), jnp.float32),
        ],
        compiler_params=pltpu.CompilerParams(vmem_limit_bytes=40 * MIB),
        cost_estimate=pl.CostEstimate(flops=60000000, bytes_accessed=6000000, transcendentals=0),
        name="y_mix",
    )(cells, weights, forward, back)


def x_back_kernel(modes, table, out, held):
    main_table, rest_table = table[0], table[1]
    for g in range(GY):
        place = GY_ORDER.index(g)
        rows = jnp.concatenate([modes[place, :, c * HQ : (c + 1) * HQ] for c in range(CM)], axis=0)
        held[pl.ds(g * HQ, HQ), :] = rows.T
    for b in range(4):
        rows = jnp.concatenate(
            [
                modes[GY_ORDER.index(4 * a + b), :, (CM + c) * HQ : (CM + c + 1) * HQ]
                for a in range(4)
                for c in range(CR)
            ],
            axis=0,
        )
        held[pl.ds(BM * 2 * KX + b * HQ, HQ), :] = rows.T
    for slot in range(BM):
        mode = slot_mode(slot)
        columns = held[pl.ds(mode * 2 * KX, 2 * KX), :]
        cells = dot(main_table, stacked_right(columns, 0), NN)
        for s in range(GX):
            out[pl.ds(s * ROWS + slot * 16, 16), :] = cells[s * 16 : (s + 1) * 16]
    for third in range(3):
        columns = held[pl.ds((BM + third) * 2 * KX, 2 * KX), :]
        cells = dot(rest_table, stacked_right(columns, 0), NN)
        for s in range(GX):
            out[pl.ds(s * ROWS + MAIN + third * 16, 16), :] = cells[s * 16 : (s + 1) * 16]


def x_back(modes, table):
    return pl.pallas_call(
        x_back_kernel,
        out_shape=jax.ShapeDtypeStruct((GX * ROWS, 128), jnp.float32),
        scratch_shapes=[pltpu.VMEM(((BM + 3) * 2 * KX, 128), jnp.float32)],
        compiler_params=pltpu.CompilerParams(vmem_limit_bytes=40 * MIB),
        cost_estimate=pl.CostEstimate(flops=150000000, bytes_accessed=2500000, transcendentals=0),
        name="x_back",
    )(modes, table)


def spread_map(channel_map):
    rows = C * RY
    copy = lax.broadcasted_iota(jnp.int32, (C, rows), 1) // RY
    copy = (copy == lax.broadcasted_iota(jnp.int32, (C, rows), 0)).astype(jnp.bfloat16)
    same = lax.broadcasted_iota(jnp.int32, (rows, rows), 0) % RY
    same = same == lax.broadcasted_iota(jnp.int32, (rows, rows), 1) % RY
    spread = []
    for half in split(channel_map):
        wide = lax.dot_general(half, copy, NN, preferred_element_type=jnp.float32)
        tall = jnp.broadcast_to(wide[:, None], (C, RY, rows)).reshape(rows, rows)
        spread.append(jnp.where(same, tall, 0.0).astype(jnp.bfloat16))
    return spread


def final_kernel(field, cells, table, channel_map, bias, out, held, left):
    high, low = spread_map(channel_map[...])
    spread = jnp.concatenate([high, high, low], axis=1)
    copies = []
    for pair in range(RX // 2):
        if pair % 2 == 0:
            tiles = jnp.stack(
                [
                    cells[pl.ds(s * ROWS + MAIN + third * 16 + (pair // 2) * 8, 8), :]
                    for s in range(GX)
                    for third in range(3)
                ]
            )
            rest = block_swap(tiles).reshape(2 * MZT, 128).T
        columns = []
        for k in range(2):
            main = jnp.concatenate(
                [cells[pl.ds(s * ROWS + 2 * pair + k, 2 * BM, stride=RX), :] for s in range(GX)],
                axis=0,
            )
            row = ((pair % 2) * 2 + k) * CR * RY
            columns += [main.T, rest[row : row + CR * RY]]
        spectral = dot(stacked_left(jnp.concatenate(columns, axis=0), 1), table[...], NN)
        for k in range(2):
            x = 2 * pair + k
            bypass = dot(spread, stacked_right(field[:, x].reshape(C * RY, ZT), 0), NN)
            value = spectral[k * C * RY : (k + 1) * C * RY] + bypass
            for c in range(C):
                one = value[c * RY : (c + 1) * RY] + bias[c]
                held[c, x] = 0.5 * one * (1.0 + lax.erf(one * np.float32(np.sqrt(0.5))))
            copies.append(pltpu.make_async_copy(held.at[:, x], out.at[:, x], left.at[x]))
            copies[-1].start()
    for copy in copies:
        copy.wait()


def final_stage(field, cells, table, channel_map, bias):
    whole = pl.BlockSpec(memory_space=pltpu.VMEM)
    return pl.pallas_call(
        final_kernel,
        in_specs=[whole, whole, whole, whole, pl.BlockSpec(memory_space=pltpu.SMEM)],
        out_specs=pl.BlockSpec(memory_space=pltpu.HBM),
        out_shape=jax.ShapeDtypeStruct((C, RX, RY, ZT), jnp.float32),
        scratch_shapes=[
            pltpu.VMEM((C, RX, RY, ZT), jnp.float32),
            pltpu.SemaphoreType.DMA((RX,)),
        ],
        compiler_params=pltpu.CompilerParams(vmem_limit_bytes=40 * MIB),
        cost_estimate=pl.CostEstimate(flops=3200000000, bytes_accessed=11000000, transcendentals=1000000),
        name="depth_back",
    )(field, cells, table, channel_map, bias)


def exchange(value, axis, groups=None):
    return lax.all_to_all(
        value, axis, split_axis=0, concat_axis=0, axis_index_groups=groups, tiled=True
    )


def shards(field, spec_weight, bypass_weight, bypass_bias):
    x_forward, x_inverse = x_tables()
    y_forward, y_inverse = y_tables()
    field = field.reshape(C, RX, RY, ZT)
    modes = depth_transform(field)
    cells = exchange(modes.reshape(GX, ROWS, 128), "gx").reshape(GX * ROWS, 128)
    pairs = exchange(x_transform(cells, x_forward), "gy", [GY_ORDER])
    mixed = exchange(mix_modes(pairs, spec_weight, y_forward, y_inverse), "gy", [GY_ORDER])
    back = x_back(mixed, x_inverse)
    back = exchange(back.reshape(GX, ROWS, 128), "gx").reshape(GX * ROWS, 128)
    out = final_stage(field, back, depth_table(), bypass_weight, bypass_bias)
    return out.reshape(1, C, RX, RY, ZT)


def solution(mesh):
    in_specs = (P(None, None, "gx", "gy", None), P(None, None, None, ("gx", "gy")), P(), P())
    out_specs = P(None, None, "gx", "gy", None)
    return jax.shard_map(shards, mesh=mesh, in_specs=in_specs, out_specs=out_specs, check_vma=False)
```

```python
import math

import jax
import jax.numpy as jnp
import ml_dtypes
import numpy as np
from jax import lax
from jax.experimental import pallas as pl
from jax.experimental.pallas import tpu as pltpu
from jax.sharding import PartitionSpec as P

C, NX, NY, NZ, NT = 20, 128, 128, 32, 24
KX, KY, KZ, KT = 24, 24, 16, 12
ZT, MZT = NZ * NT, KZ * KT
GX = GY = 16
RX, RY = NX // GX, NY // GY
BM = MZT // GX
H = BM * KX // GY
HQ = 2 * H
CM, CR = 16, 4
MAIN = BM * 2 * RX
ROWS = MAIN + BM * 2 * RX * CR // CM
HALF = ZT // 2
LANES = 768
MIB = 1024 * 1024

NN = (((1,), (0,)), ((), ()))
NT_DIMS = (((1,), (1,)), ((), ()))


GY_ORDER = [x * 4 + z for z in range(4) for x in range(4)]


def slot_mode(slot):
    return (slot % 4) * 3 + slot // 4


def kept(count, length):
    steps = np.arange(count)
    return np.where(steps < count // 2, steps, length - count + steps)


def halves(table):
    table = table.astype(np.float32)
    high = table.astype(ml_dtypes.bfloat16)
    low = (table - high.astype(np.float32)).astype(ml_dtypes.bfloat16)
    return np.stack([high, low])


def depth_table():
    kz = kept(KZ, NZ)
    modes = np.array([g * BM + slot_mode(s) for g in range(GX) for s in range(BM)])
    z_freq, t_freq = kz[modes // KT], modes % KT
    cells = np.arange(ZT)
    turns = (z_freq[:, None] * (cells // NT)[None] * NT + t_freq[:, None] * (cells % NT)[None] * NZ) % ZT
    angle = turns * (2.0 * np.pi / ZT)
    cosine, sine = np.cos(angle), np.sin(angle)
    scale = (np.where(t_freq == 0, 1.0, 2.0) / (NX * NY * ZT))[:, None]
    inverse = np.stack([cosine * scale, -sine * scale], axis=1).reshape(2 * MZT, ZT)
    return right_table(inverse)


def x_tables():
    angle = (np.arange(NX)[:, None] * kept(KX, NX)[None] % NX) * (2.0 * np.pi / NX)
    cosine, sine = np.cos(angle), np.sin(angle)
    forward = np.stack([np.stack([cosine, -sine], -1), np.stack([sine, cosine], -1)], 1)
    back = np.stack([np.stack([cosine, -sine], -1), np.stack([sine, cosine], -1)], 1)
    shape = (GX, RX, 2, KX * 2)
    forward, back = forward.reshape(shape), back.reshape(shape)
    def main(table):
        return table.transpose(0, 2, 1, 3).reshape(GX * 2 * RX, KX * 2)
    def rest(table):
        return table.reshape(GX * RX * 2, KX * 2)
    return (
        np.stack([left_table(main(forward).T), left_table(rest(forward).T)]),
        np.stack([left_table(main(back)), left_table(rest(back))]),
    )


def y_tables():
    angle = (np.arange(NY)[:, None] * kept(KY, NY)[None] % NY) * (2.0 * np.pi / NY)
    cosine, sine = np.cos(angle), np.sin(angle)
    both = np.concatenate([cosine, sine], axis=1)
    both = both.reshape(GY, RY, 2 * KY)[np.array(GY_ORDER)].reshape(NY, 2 * KY)
    return left_table(both.T), left_table(both)


def split(value):
    high = value.astype(jnp.bfloat16)
    return high, (value - high.astype(jnp.float32)).astype(jnp.bfloat16)


def stacked_left(value, axis):
    high, low = split(value)
    return jnp.concatenate([high, high, low], axis=axis)


def stacked_right(value, axis):
    high, low = split(value)
    return jnp.concatenate([high, low, high], axis=axis)


def left_table(table):
    high, low = halves(table)
    return np.concatenate([high, high, low], axis=1)


def right_table(table):
    high, low = halves(table)
    return np.concatenate([high, low, high], axis=0)


def dot(left, right, dims):
    return lax.dot_general(left, right, dims, preferred_element_type=jnp.float32)


def block_swap(value):
    row = lax.broadcasted_iota(jnp.int32, value.shape, 1) // 2
    lane = lax.broadcasted_iota(jnp.int32, value.shape, 2) // 32
    far = pltpu.roll(pltpu.roll(value, 4, 1), 64, 2)
    value = jnp.where((row // 2) == (lane // 2), value, far)
    up = pltpu.roll(pltpu.roll(value, 6, 1), 32, 2)
    down = pltpu.roll(pltpu.roll(value, 2, 1), 96, 2)
    return jnp.where((row % 2) == (lane % 2), value, jnp.where(row % 2 == 0, up, down))


def divide(value, by):
    return (value * 2731) >> 16 if by == 24 else value // by


def cos_sin(index, length):
    half = (index - length // 2).astype(jnp.float32) * np.float32(np.pi / length)
    square = half * half
    sine, cosine = jnp.zeros_like(half), jnp.zeros_like(half)
    for power in range(14, -1, -2):
        sign = -1.0 if power % 4 else 1.0
        cosine = cosine * square + np.float32(sign / math.factorial(power))
        sine = sine * square + np.float32(sign / math.factorial(power + 1))
    sine = sine * half
    return 2.0 * sine * sine - 1.0, -2.0 * sine * cosine


def fill_forward_table(table):
    def cells(rows):
        row = lax.broadcasted_iota(jnp.int32, (rows, HALF), 0)
        lane = lax.broadcasted_iota(jnp.int32, (rows, HALF), 1)
        z = divide(lane, NT)
        return row, z, lane - NT * z
    row, z, _ = cells(GX)
    z_freq = jnp.where(row < KZ // 2, row, row + NZ - KZ)
    z_cos, z_sin = cos_sin((z_freq * z) % NZ, NZ)
    row, _, t = cells(2 * BM)
    slot = row >> 1
    turns = ((slot & 3) * 3 + (slot >> 2)) * t
    t_cos, t_sin = cos_sin(turns - NT * divide(turns, NT), NT)
    real = (row & 1) == 0
    one = jnp.where(real, t_cos, -t_sin)
    two = jnp.where(real, -t_sin, -t_cos)
    for odd in range(2):
        rows = [z_cos[g : g + 1] * one + z_sin[g : g + 1] * two for g in range(odd, GX, 2)]
        table[odd] = jnp.concatenate(split(jnp.concatenate(rows, axis=0)), axis=0)


def depth_modes(cells, table):
    near, far = cells[:, :HALF], cells[:, HALF:]
    modes = []
    for odd in range(2):
        high, low = split(near - far if odd else near + far)
        both = dot(table[odd], high, NT_DIMS)
        modes.append(both[:MZT] + (both[MZT:] + dot(table[odd, :MZT], low, NT_DIMS)))
    return modes


def depth_kernel(field, out, held, table, arrived):
    copies = [
        pltpu.make_async_copy(field.at[:, pl.ds(2 * pair, 2)], held.at[pair], arrived.at[pair])
        for pair in range(4)
    ]
    for copy in copies:
        copy.start()
    fill_forward_table(table)
    for pair in range(4):
        if pair < 2:
            for copy in copies[pair : 1 + 3 * pair]:
                copy.wait()
        cells = jnp.concatenate(
            [held[pair, 0:CM, k].reshape(CM * RY, ZT) for k in range(2)], axis=0
        )
        modes = depth_modes(cells, table)
        for k in range(2):
            for dest in range(GX):
                start = dest * ROWS + 2 * pair + k
                row = dest // 2 * 2 * BM
                out[pl.ds(start, 2 * BM, stride=RX), :] = modes[dest % 2][
                    row : row + 2 * BM, k * 128 : (k + 1) * 128
                ]
    cells = jnp.concatenate(
        [held[k // 2, CM:C, k % 2].reshape(CR * RY, ZT) for k in range(RX)], axis=0
    )
    modes = depth_modes(cells, table)
    for half in range(2):
        for odd in range(2):
            tiles = block_swap(modes[odd][:, half * 128 : (half + 1) * 128].reshape(GX // 2 * 3, 8, 128))
            for dest in range(odd, GX, 2):
                for third in range(3):
                    start = dest * ROWS + MAIN + third * 16 + half * 8
                    out[pl.ds(start, 8), :] = tiles[dest // 2 * 3 + third]


def depth_transform(field):
    return pl.pallas_call(
        depth_kernel,
        in_specs=[pl.BlockSpec(memory_space=pltpu.HBM)],
        out_shape=jax.ShapeDtypeStruct((GX * ROWS, 128), jnp.float32),
        scratch_shapes=[
            pltpu.VMEM((4, C, 2, RY, ZT), jnp.float32),
            pltpu.VMEM((2, 2 * MZT, HALF), jnp.bfloat16),
            pltpu.SemaphoreType.DMA((4,)),
        ],
        compiler_params=pltpu.CompilerParams(vmem_limit_bytes=50 * MIB),
        cost_estimate=pl.CostEstimate(flops=1200000000, bytes_accessed=6000000, transcendentals=0),
        name="depth_forward",
    )(field)


def x_kernel(cells, table, out, held):
    main_table, rest_table = table[0], table[1]
    for slot in range(BM):
        columns = jnp.concatenate(
            [cells[pl.ds(s * ROWS + slot * 16, 16), :] for s in range(GX)], axis=0
        )
        mode = slot_mode(slot)
        held[pl.ds(mode * 2 * KX, 2 * KX), :] = dot(main_table, stacked_right(columns, 0), NN)
    for third in range(3):
        columns = jnp.concatenate(
            [cells[pl.ds(s * ROWS + MAIN + third * 16, 16), :] for s in range(GX)], axis=0
        )
        held[pl.ds((BM + third) * 2 * KX, 2 * KX), :] = dot(rest_table, stacked_right(columns, 0), NN)
    for g in range(GY):
        place = GY_ORDER.index(g)
        turned = held[pl.ds(g * HQ, HQ), :].T
        for c in range(CM):
            out[place, :, c * HQ : (c + 1) * HQ] = turned[c * RY : (c + 1) * RY]
    for b in range(4):
        turned = held[pl.ds(BM * 2 * KX + b * HQ, HQ), :].T
        for a in range(4):
            for c in range(CR):
                row = (a * CR + c) * RY
                out[GY_ORDER.index(4 * a + b), :, (CM + c) * HQ : (CM + c + 1) * HQ] = turned[row : row + RY]
    for g in range(GY):
        out[g, :, C * HQ : LANES] = jnp.zeros((RY, LANES - C * HQ), jnp.float32)


def x_transform(cells, table):
    return pl.pallas_call(
        x_kernel,
        out_shape=jax.ShapeDtypeStruct((GY, RY, LANES), jnp.float32),
        scratch_shapes=[pltpu.VMEM(((BM + 3) * 2 * KX, 128), jnp.float32)],
        compiler_params=pltpu.CompilerParams(vmem_limit_bytes=40 * MIB),
        cost_estimate=pl.CostEstimate(flops=150000000, bytes_accessed=2500000, transcendentals=0),
        name="x_forward",
    )(cells, table)


def even_lanes(shape):
    return lax.broadcasted_iota(jnp.int32, shape, len(shape) - 1) % 2 == 0


def turn_parts(value, even):
    lanes = value.shape[-1]
    return jnp.where(even, -pltpu.roll(value, lanes - 1, 1), pltpu.roll(value, 1, 1))


def mix_kernel(cells, weights, forward, back, out, reals, imags, mixed):
    sums = dot(forward[...], stacked_right(cells[...].reshape(GY * RY, LANES), 0), NN)
    even = even_lanes((KY, LANES))
    coef = sums[:KY] - turn_parts(sums[KY:], even)
    real = jnp.where(even, coef, pltpu.roll(coef, 1, 1))
    imag = jnp.where(even, pltpu.roll(coef, LANES - 1, 1), coef)
    for i in range(C):
        reals[i] = real[:, i * HQ : (i + 1) * HQ]
        imags[i] = imag[:, i * HQ : (i + 1) * HQ]
    even_pairs = even_lanes((KY, HQ))
    group = 4
    for first in range(0, C, group):
        one = [jnp.zeros((KY, HQ), jnp.float32)] * group
        two = [jnp.zeros((KY, HQ), jnp.float32)] * group
        for i in range(C):
            real_i, imag_i = reals[i], imags[i]
            for k in range(group):
                weight = weights[i, first + k]
                one[k] = one[k] + weight * real_i
                two[k] = two[k] + weight * imag_i
        for k in range(group):
            o = first + k
            mixed[:, o * HQ : (o + 1) * HQ] = one[k] + turn_parts(two[k], even_pairs)
    mixed[:, C * HQ : LANES] = jnp.zeros((KY, LANES - C * HQ), jnp.float32)
    modes = mixed[...]
    both = jnp.concatenate([modes, turn_parts(modes, even)], axis=0)
    out[...] = dot(back[...], stacked_right(both, 0), NN).reshape(GY, RY, LANES)


def mix_modes(cells, weights, forward, back):
    return pl.pallas_call(
        mix_kernel,
        out_shape=jax.ShapeDtypeStruct((GY, RY, LANES), jnp.float32),
        scratch_shapes=[
            pltpu.VMEM((C, KY, HQ), jnp.float32),
            pltpu.VMEM((C, KY, HQ), jnp.float32),
            pltpu.VMEM((KY, LANES), jnp.float32),
        ],
        compiler_params=pltpu.CompilerParams(vmem_limit_bytes=40 * MIB),
        cost_estimate=pl.CostEstimate(flops=60000000, bytes_accessed=6000000, transcendentals=0),
        name="y_mix",
    )(cells, weights, forward, back)


def x_back_kernel(modes, table, out, held):
    main_table, rest_table = table[0], table[1]
    for g in range(GY):
        place = GY_ORDER.index(g)
        rows = jnp.concatenate([modes[place, :, c * HQ : (c + 1) * HQ] for c in range(CM)], axis=0)
        held[pl.ds(g * HQ, HQ), :] = rows.T
    for b in range(4):
        rows = jnp.concatenate(
            [
                modes[GY_ORDER.index(4 * a + b), :, (CM + c) * HQ : (CM + c + 1) * HQ]
                for a in range(4)
                for c in range(CR)
            ],
            axis=0,
        )
        held[pl.ds(BM * 2 * KX + b * HQ, HQ), :] = rows.T
    for slot in range(BM):
        mode = slot_mode(slot)
        columns = held[pl.ds(mode * 2 * KX, 2 * KX), :]
        cells = dot(main_table, stacked_right(columns, 0), NN)
        for s in range(GX):
            out[pl.ds(s * ROWS + slot * 16, 16), :] = cells[s * 16 : (s + 1) * 16]
    for third in range(3):
        columns = held[pl.ds((BM + third) * 2 * KX, 2 * KX), :]
        cells = dot(rest_table, stacked_right(columns, 0), NN)
        for s in range(GX):
            out[pl.ds(s * ROWS + MAIN + third * 16, 16), :] = cells[s * 16 : (s + 1) * 16]


def x_back(modes, table):
    return pl.pallas_call(
        x_back_kernel,
        out_shape=jax.ShapeDtypeStruct((GX * ROWS, 128), jnp.float32),
        scratch_shapes=[pltpu.VMEM(((BM + 3) * 2 * KX, 128), jnp.float32)],
        compiler_params=pltpu.CompilerParams(vmem_limit_bytes=40 * MIB),
        cost_estimate=pl.CostEstimate(flops=150000000, bytes_accessed=2500000, transcendentals=0),
        name="x_back",
    )(modes, table)


def spread_map(channel_map):
    rows = C * RY
    copy = lax.broadcasted_iota(jnp.int32, (C, rows), 1) // RY
    copy = (copy == lax.broadcasted_iota(jnp.int32, (C, rows), 0)).astype(jnp.bfloat16)
    same = lax.broadcasted_iota(jnp.int32, (rows, rows), 0) % RY
    same = same == lax.broadcasted_iota(jnp.int32, (rows, rows), 1) % RY
    spread = []
    for half in split(channel_map):
        wide = lax.dot_general(half, copy, NN, preferred_element_type=jnp.float32)
        tall = jnp.broadcast_to(wide[:, None], (C, RY, rows)).reshape(rows, rows)
        spread.append(jnp.where(same, tall, 0.0).astype(jnp.bfloat16))
    return spread


def final_kernel(field, cells, table, channel_map, bias, out, held, left):
    high, low = spread_map(channel_map[...])
    spread = jnp.concatenate([high, high, low], axis=1)
    copies = []
    for pair in range(RX // 2):
        if pair % 2 == 0:
            tiles = jnp.stack(
                [
                    cells[pl.ds(s * ROWS + MAIN + third * 16 + (pair // 2) * 8, 8), :]
                    for s in range(GX)
                    for third in range(3)
                ]
            )
            rest = block_swap(tiles).reshape(2 * MZT, 128).T
        columns = []
        for k in range(2):
            main = jnp.concatenate(
                [cells[pl.ds(s * ROWS + 2 * pair + k, 2 * BM, stride=RX), :] for s in range(GX)],
                axis=0,
            )
            row = ((pair % 2) * 2 + k) * CR * RY
            columns += [main.T, rest[row : row + CR * RY]]
        spectral = dot(stacked_left(jnp.concatenate(columns, axis=0), 1), table[...], NN)
        for k in range(2):
            x = 2 * pair + k
            bypass = dot(spread, stacked_right(field[:, x].reshape(C * RY, ZT), 0), NN)
            value = spectral[k * C * RY : (k + 1) * C * RY] + bypass
            for c in range(C):
                one = value[c * RY : (c + 1) * RY] + bias[c]
                held[c, x] = 0.5 * one * (1.0 + lax.erf(one * np.float32(np.sqrt(0.5))))
            copies.append(pltpu.make_async_copy(held.at[:, x], out.at[:, x], left.at[x]))
            copies[-1].start()
    for copy in copies:
        copy.wait()


def final_stage(field, cells, table, channel_map, bias):
    whole = pl.BlockSpec(memory_space=pltpu.VMEM)
    return pl.pallas_call(
        final_kernel,
        in_specs=[whole, whole, whole, whole, pl.BlockSpec(memory_space=pltpu.SMEM)],
        out_specs=pl.BlockSpec(memory_space=pltpu.HBM),
        out_shape=jax.ShapeDtypeStruct((C, RX, RY, ZT), jnp.float32),
        scratch_shapes=[
            pltpu.VMEM((C, RX, RY, ZT), jnp.float32),
            pltpu.SemaphoreType.DMA((RX,)),
        ],
        compiler_params=pltpu.CompilerParams(vmem_limit_bytes=40 * MIB),
        cost_estimate=pl.CostEstimate(flops=3200000000, bytes_accessed=11000000, transcendentals=1000000),
        name="depth_back",
    )(field, cells, table, channel_map, bias)


def exchange(value, axis, groups=None):
    return lax.all_to_all(
        value, axis, split_axis=0, concat_axis=0, axis_index_groups=groups, tiled=True
    )


def shards(field, spec_weight, bypass_weight, bypass_bias):
    x_forward, x_inverse = x_tables()
    y_forward, y_inverse = y_tables()
    field = field.reshape(C, RX, RY, ZT)
    modes = depth_transform(field)
    cells = exchange(modes.reshape(GX, ROWS, 128), "gx").reshape(GX * ROWS, 128)
    pairs = exchange(x_transform(cells, x_forward), "gy", [GY_ORDER])
    mixed = exchange(mix_modes(pairs, spec_weight, y_forward, y_inverse), "gy", [GY_ORDER])
    back = x_back(mixed, x_inverse)
    back = exchange(back.reshape(GX, ROWS, 128), "gx").reshape(GX * ROWS, 128)
    out = final_stage(field, back, depth_table(), bypass_weight, bypass_bias)
    return out.reshape(1, C, RX, RY, ZT)


def solution(mesh):
    in_specs = (P(None, None, "gx", "gy", None), P(None, None, None, ("gx", "gy")), P(), P())
    out_specs = P(None, None, "gx", "gy", None)
    return jax.shard_map(shards, mesh=mesh, in_specs=in_specs, out_specs=out_specs, check_vma=False)
```

```python
import math

import jax
import jax.numpy as jnp
import ml_dtypes
import numpy as np
from jax import lax
from jax.experimental import pallas as pl
from jax.experimental.pallas import tpu as pltpu
from jax.sharding import PartitionSpec as P

C, NX, NY, NZ, NT = 20, 128, 128, 32, 24
KX, KY, KZ, KT = 24, 24, 16, 12
ZT, MZT = NZ * NT, KZ * KT
GX = GY = 16
RX, RY = NX // GX, NY // GY
BM = MZT // GX
H = BM * KX // GY
HQ = 2 * H
CM, CR = 16, 4
MAIN = BM * 2 * RX
ROWS = MAIN + BM * 2 * RX * CR // CM
HALF = ZT // 2
LANES = 768
MIB = 1024 * 1024

NN = (((1,), (0,)), ((), ()))
NT_DIMS = (((1,), (1,)), ((), ()))


GY_ORDER = [x * 4 + z for z in range(4) for x in range(4)]


def slot_mode(slot):
    return (slot % 4) * 3 + slot // 4


def kept(count, length):
    steps = np.arange(count)
    return np.where(steps < count // 2, steps, length - count + steps)


def halves(table):
    table = table.astype(np.float32)
    high = table.astype(ml_dtypes.bfloat16)
    low = (table - high.astype(np.float32)).astype(ml_dtypes.bfloat16)
    return np.stack([high, low])


def depth_table():
    kz = kept(KZ, NZ)
    modes = np.array([g * BM + slot_mode(s) for g in range(GX) for s in range(BM)])
    z_freq, t_freq = kz[modes // KT], modes % KT
    cells = np.arange(ZT)
    turns = (z_freq[:, None] * (cells // NT)[None] * NT + t_freq[:, None] * (cells % NT)[None] * NZ) % ZT
    angle = turns * (2.0 * np.pi / ZT)
    cosine, sine = np.cos(angle), np.sin(angle)
    scale = (np.where(t_freq == 0, 1.0, 2.0) / (NX * NY * ZT))[:, None]
    inverse = np.stack([cosine * scale, -sine * scale], axis=1).reshape(2 * MZT, ZT)
    return right_table(inverse)


def x_tables():
    angle = (np.arange(NX)[:, None] * kept(KX, NX)[None] % NX) * (2.0 * np.pi / NX)
    cosine, sine = np.cos(angle), np.sin(angle)
    forward = np.stack([np.stack([cosine, -sine], -1), np.stack([sine, cosine], -1)], 1)
    back = np.stack([np.stack([cosine, -sine], -1), np.stack([sine, cosine], -1)], 1)
    shape = (GX, RX, 2, KX * 2)
    forward, back = forward.reshape(shape), back.reshape(shape)
    def main(table):
        return table.transpose(0, 2, 1, 3).reshape(GX * 2 * RX, KX * 2)
    def rest(table):
        return table.reshape(GX * RX * 2, KX * 2)
    return (
        np.stack([left_table(main(forward).T), left_table(rest(forward).T)]),
        np.stack([left_table(main(back)), left_table(rest(back))]),
    )


def y_tables():
    angle = (np.arange(NY)[:, None] * kept(KY, NY)[None] % NY) * (2.0 * np.pi / NY)
    cosine, sine = np.cos(angle), np.sin(angle)
    both = np.concatenate([cosine, sine], axis=1)
    both = both.reshape(GY, RY, 2 * KY)[np.array(GY_ORDER)].reshape(NY, 2 * KY)
    return left_table(both.T), left_table(both)


def split(value):
    high = value.astype(jnp.bfloat16)
    return high, (value - high.astype(jnp.float32)).astype(jnp.bfloat16)


def stacked_left(value, axis):
    high, low = split(value)
    return jnp.concatenate([high, high, low], axis=axis)


def stacked_right(value, axis):
    high, low = split(value)
    return jnp.concatenate([high, low, high], axis=axis)


def left_table(table):
    high, low = halves(table)
    return np.concatenate([high, high, low], axis=1)


def right_table(table):
    high, low = halves(table)
    return np.concatenate([high, low, high], axis=0)


def dot(left, right, dims):
    return lax.dot_general(left, right, dims, preferred_element_type=jnp.float32)


def block_swap(value):
    row = lax.broadcasted_iota(jnp.int32, value.shape, 1) // 2
    lane = lax.broadcasted_iota(jnp.int32, value.shape, 2) // 32
    far = pltpu.roll(pltpu.roll(value, 4, 1), 64, 2)
    value = jnp.where((row // 2) == (lane // 2), value, far)
    up = pltpu.roll(pltpu.roll(value, 6, 1), 32, 2)
    down = pltpu.roll(pltpu.roll(value, 2, 1), 96, 2)
    return jnp.where((row % 2) == (lane % 2), value, jnp.where(row % 2 == 0, up, down))


def divide(value, by):
    return (value * 2731) >> 16 if by == 24 else value // by


def cos_sin(index, length):
    half = (index - length // 2).astype(jnp.float32) * np.float32(np.pi / length)
    square = half * half
    sine, cosine = jnp.zeros_like(half), jnp.zeros_like(half)
    for power in range(14, -1, -2):
        sign = -1.0 if power % 4 else 1.0
        cosine = cosine * square + np.float32(sign / math.factorial(power))
        sine = sine * square + np.float32(sign / math.factorial(power + 1))
    sine = sine * half
    return 2.0 * sine * sine - 1.0, -2.0 * sine * cosine


def fill_forward_table(table):
    def cells(rows):
        row = lax.broadcasted_iota(jnp.int32, (rows, HALF), 0)
        lane = lax.broadcasted_iota(jnp.int32, (rows, HALF), 1)
        z = divide(lane, NT)
        return row, z, lane - NT * z
    row, z, _ = cells(GX)
    z_freq = jnp.where(row < KZ // 2, row, row + NZ - KZ)
    z_cos, z_sin = cos_sin((z_freq * z) % NZ, NZ)
    row, _, t = cells(2 * BM)
    slot = row >> 1
    turns = ((slot & 3) * 3 + (slot >> 2)) * t
    t_cos, t_sin = cos_sin(turns - NT * divide(turns, NT), NT)
    real = (row & 1) == 0
    one = jnp.where(real, t_cos, -t_sin)
    two = jnp.where(real, -t_sin, -t_cos)
    for odd in range(2):
        rows = [z_cos[g : g + 1] * one + z_sin[g : g + 1] * two for g in range(odd, GX, 2)]
        table[odd] = jnp.concatenate(split(jnp.concatenate(rows, axis=0)), axis=0)


def depth_modes(cells, table):
    near, far = cells[:, :HALF], cells[:, HALF:]
    modes = []
    for odd in range(2):
        high, low = split(near - far if odd else near + far)
        both = dot(table[odd], high, NT_DIMS)
        modes.append(both[:MZT] + (both[MZT:] + dot(table[odd, :MZT], low, NT_DIMS)))
    return modes


def depth_kernel(field, out, held, table, arrived):
    copies = [
        pltpu.make_async_copy(field.at[:, pl.ds(2 * pair, 2)], held.at[pair], arrived.at[pair])
        for pair in range(4)
    ]
    for copy in copies:
        copy.start()
    fill_forward_table(table)
    for pair in range(4):
        if pair < 2:
            for copy in copies[pair : 1 + 3 * pair]:
                copy.wait()
        cells = jnp.concatenate(
            [held[pair, 0:CM, k].reshape(CM * RY, ZT) for k in range(2)], axis=0
        )
        modes = depth_modes(cells, table)
        for k in range(2):
            for dest in range(GX):
                start = dest * ROWS + 2 * pair + k
                row = dest // 2 * 2 * BM
                out[pl.ds(start, 2 * BM, stride=RX), :] = modes[dest % 2][
                    row : row + 2 * BM, k * 128 : (k + 1) * 128
                ]
    cells = jnp.concatenate(
        [held[k // 2, CM:C, k % 2].reshape(CR * RY, ZT) for k in range(RX)], axis=0
    )
    modes = depth_modes(cells, table)
    for half in range(2):
        for odd in range(2):
            tiles = block_swap(modes[odd][:, half * 128 : (half + 1) * 128].reshape(GX // 2 * 3, 8, 128))
            for dest in range(odd, GX, 2):
                for third in range(3):
                    start = dest * ROWS + MAIN + third * 16 + half * 8
                    out[pl.ds(start, 8), :] = tiles[dest // 2 * 3 + third]


def depth_transform(field):
    return pl.pallas_call(
        depth_kernel,
        in_specs=[pl.BlockSpec(memory_space=pltpu.HBM)],
        out_shape=jax.ShapeDtypeStruct((GX * ROWS, 128), jnp.float32),
        scratch_shapes=[
            pltpu.VMEM((4, C, 2, RY, ZT), jnp.float32),
            pltpu.VMEM((2, 2 * MZT, HALF), jnp.bfloat16),
            pltpu.SemaphoreType.DMA((4,)),
        ],
        compiler_params=pltpu.CompilerParams(vmem_limit_bytes=50 * MIB),
        cost_estimate=pl.CostEstimate(flops=1200000000, bytes_accessed=6000000, transcendentals=0),
        name="depth_forward",
    )(field)


def x_kernel(cells, table, out):
    def modes_of(first, which):
        columns = jnp.concatenate(
            [cells[pl.ds(s * ROWS + first, 16), :] for s in range(GX)], axis=0
        )
        return dot(table[which], stacked_right(columns, 0), NN)

    slots = [0] * BM
    for slot in range(BM):
        slots[slot_mode(slot)] = slot
    for a in range(4):
        modes = jnp.concatenate([modes_of(slots[3 * a + m] * 16, 0) for m in range(3)], axis=0)
        for b in range(4):
            place = GY_ORDER.index(4 * a + b)
            turned = modes[b * HQ : (b + 1) * HQ].T
            for c in range(CM):
                out[place, :, c * HQ : (c + 1) * HQ] = turned[c * RY : (c + 1) * RY]
    modes = jnp.concatenate([modes_of(MAIN + m * 16, 1) for m in range(3)], axis=0)
    for b in range(4):
        turned = modes[b * HQ : (b + 1) * HQ].T
        for a in range(4):
            place = GY_ORDER.index(4 * a + b)
            for c in range(CR):
                row = (a * CR + c) * RY
                out[place, :, (CM + c) * HQ : (CM + c + 1) * HQ] = turned[row : row + RY]
            out[place, :, C * HQ : LANES] = jnp.zeros((RY, LANES - C * HQ), jnp.float32)


def x_transform(cells, table):
    return pl.pallas_call(
        x_kernel,
        out_shape=jax.ShapeDtypeStruct((GY, RY, LANES), jnp.float32),
        compiler_params=pltpu.CompilerParams(vmem_limit_bytes=40 * MIB),
        cost_estimate=pl.CostEstimate(flops=150000000, bytes_accessed=2500000, transcendentals=0),
        name="x_forward",
    )(cells, table)


def even_lanes(shape):
    return lax.broadcasted_iota(jnp.int32, shape, len(shape) - 1) % 2 == 0


def turn_parts(value, even):
    lanes = value.shape[-1]
    return jnp.where(even, -pltpu.roll(value, lanes - 1, 1), pltpu.roll(value, 1, 1))


def mix_kernel(cells, weights, forward, back, out, reals, imags, mixed):
    sums = dot(forward[...], stacked_right(cells[...].reshape(GY * RY, LANES), 0), NN)
    even = even_lanes((KY, LANES))
    coef = sums[:KY] - turn_parts(sums[KY:], even)
    real = jnp.where(even, coef, pltpu.roll(coef, 1, 1))
    imag = jnp.where(even, pltpu.roll(coef, LANES - 1, 1), coef)
    for i in range(C):
        reals[i] = real[:, i * HQ : (i + 1) * HQ]
        imags[i] = imag[:, i * HQ : (i + 1) * HQ]
    even_pairs = even_lanes((KY, HQ))
    group = 4
    for first in range(0, C, group):
        one = [jnp.zeros((KY, HQ), jnp.float32)] * group
        two = [jnp.zeros((KY, HQ), jnp.float32)] * group
        for i in range(C):
            real_i, imag_i = reals[i], imags[i]
            for k in range(group):
                weight = weights[i, first + k]
                one[k] = one[k] + weight * real_i
                two[k] = two[k] + weight * imag_i
        for k in range(group):
            o = first + k
            mixed[:, o * HQ : (o + 1) * HQ] = one[k] + turn_parts(two[k], even_pairs)
    mixed[:, C * HQ : LANES] = jnp.zeros((KY, LANES - C * HQ), jnp.float32)
    modes = mixed[...]
    both = jnp.concatenate([modes, turn_parts(modes, even)], axis=0)
    out[...] = dot(back[...], stacked_right(both, 0), NN).reshape(GY, RY, LANES)


def mix_modes(cells, weights, forward, back):
    return pl.pallas_call(
        mix_kernel,
        out_shape=jax.ShapeDtypeStruct((GY, RY, LANES), jnp.float32),
        scratch_shapes=[
            pltpu.VMEM((C, KY, HQ), jnp.float32),
            pltpu.VMEM((C, KY, HQ), jnp.float32),
            pltpu.VMEM((KY, LANES), jnp.float32),
        ],
        compiler_params=pltpu.CompilerParams(vmem_limit_bytes=40 * MIB),
        cost_estimate=pl.CostEstimate(flops=60000000, bytes_accessed=6000000, transcendentals=0),
        name="y_mix",
    )(cells, weights, forward, back)


def x_back_kernel(modes, table, out):
    def write(first, which, columns):
        cells = dot(table[which], stacked_right(columns, 0), NN)
        for s in range(GX):
            out[pl.ds(s * ROWS + first, 16), :] = cells[s * 16 : (s + 1) * 16]

    def columns_of(pieces):
        rows = jnp.concatenate(
            [modes[GY_ORDER.index(g), :, c * HQ : (c + 1) * HQ] for g, c in pieces], axis=0
        )
        return rows.T

    slots = [0] * BM
    for slot in range(BM):
        slots[slot_mode(slot)] = slot
    for a in range(4):
        parts = [columns_of([(4 * a + b, c) for c in range(CM)]) for b in range(4)]
        columns = jnp.concatenate(parts, axis=0)
        for m in range(3):
            write(slots[3 * a + m] * 16, 0, columns[m * 2 * KX : (m + 1) * 2 * KX])
    parts = [
        columns_of([(4 * a + b, CM + c) for a in range(4) for c in range(CR)]) for b in range(4)
    ]
    columns = jnp.concatenate(parts, axis=0)
    for m in range(3):
        write(MAIN + m * 16, 1, columns[m * 2 * KX : (m + 1) * 2 * KX])


def x_back(modes, table):
    return pl.pallas_call(
        x_back_kernel,
        out_shape=jax.ShapeDtypeStruct((GX * ROWS, 128), jnp.float32),
        compiler_params=pltpu.CompilerParams(vmem_limit_bytes=40 * MIB),
        cost_estimate=pl.CostEstimate(flops=150000000, bytes_accessed=2500000, transcendentals=0),
        name="x_back",
    )(modes, table)


def spread_map(channel_map):
    rows = C * RY
    copy = lax.broadcasted_iota(jnp.int32, (C, rows), 1) // RY
    copy = (copy == lax.broadcasted_iota(jnp.int32, (C, rows), 0)).astype(jnp.bfloat16)
    same = lax.broadcasted_iota(jnp.int32, (rows, rows), 0) % RY
    same = same == lax.broadcasted_iota(jnp.int32, (rows, rows), 1) % RY
    spread = []
    for half in split(channel_map):
        wide = lax.dot_general(half, copy, NN, preferred_element_type=jnp.float32)
        tall = jnp.broadcast_to(wide[:, None], (C, RY, rows)).reshape(rows, rows)
        spread.append(jnp.where(same, tall, 0.0).astype(jnp.bfloat16))
    return spread


def final_kernel(field, cells, table, channel_map, bias, out, held, left):
    high, low = spread_map(channel_map[...])
    spread = jnp.concatenate([high, high, low], axis=1)
    copies = []
    for pair in range(RX // 2):
        if pair % 2 == 0:
            tiles = jnp.stack(
                [
                    cells[pl.ds(s * ROWS + MAIN + third * 16 + (pair // 2) * 8, 8), :]
                    for s in range(GX)
                    for third in range(3)
                ]
            )
            rest = block_swap(tiles).reshape(2 * MZT, 128).T
        columns = []
        for k in range(2):
            main = jnp.concatenate(
                [cells[pl.ds(s * ROWS + 2 * pair + k, 2 * BM, stride=RX), :] for s in range(GX)],
                axis=0,
            )
            row = ((pair % 2) * 2 + k) * CR * RY
            columns += [main.T, rest[row : row + CR * RY]]
        spectral = dot(stacked_left(jnp.concatenate(columns, axis=0), 1), table[...], NN)
        for k in range(2):
            x = 2 * pair + k
            bypass = dot(spread, stacked_right(field[:, x].reshape(C * RY, ZT), 0), NN)
            value = spectral[k * C * RY : (k + 1) * C * RY] + bypass
            for c in range(C):
                one = value[c * RY : (c + 1) * RY] + bias[c]
                held[c, x] = 0.5 * one * (1.0 + lax.erf(one * np.float32(np.sqrt(0.5))))
                first = C // 2 if x == RX - 1 and c >= C // 2 else 0
                if c == C - 1 or (x == RX - 1 and c == C // 2 - 1):
                    part = pl.ds(first, c + 1 - first)
                    copy = pltpu.make_async_copy(
                        held.at[part, x], out.at[part, x], left.at[len(copies)]
                    )
                    copies.append(copy)
                    copy.start()
    for copy in copies:
        copy.wait()


def final_stage(field, cells, table, channel_map, bias):
    whole = pl.BlockSpec(memory_space=pltpu.VMEM)
    return pl.pallas_call(
        final_kernel,
        in_specs=[whole, whole, whole, whole, pl.BlockSpec(memory_space=pltpu.SMEM)],
        out_specs=pl.BlockSpec(memory_space=pltpu.HBM),
        out_shape=jax.ShapeDtypeStruct((C, RX, RY, ZT), jnp.float32),
        scratch_shapes=[
            pltpu.VMEM((C, RX, RY, ZT), jnp.float32),
            pltpu.SemaphoreType.DMA((RX + 1,)),
        ],
        compiler_params=pltpu.CompilerParams(vmem_limit_bytes=40 * MIB),
        cost_estimate=pl.CostEstimate(flops=3200000000, bytes_accessed=11000000, transcendentals=1000000),
        name="depth_back",
    )(field, cells, table, channel_map, bias)


def exchange(value, axis, groups=None):
    return lax.all_to_all(
        value, axis, split_axis=0, concat_axis=0, axis_index_groups=groups, tiled=True
    )


def shards(field, spec_weight, bypass_weight, bypass_bias):
    x_forward, x_inverse = x_tables()
    y_forward, y_inverse = y_tables()
    field = field.reshape(C, RX, RY, ZT)
    modes = depth_transform(field)
    cells = exchange(modes.reshape(GX, ROWS, 128), "gx").reshape(GX * ROWS, 128)
    pairs = exchange(x_transform(cells, x_forward), "gy", [GY_ORDER])
    mixed = exchange(mix_modes(pairs, spec_weight, y_forward, y_inverse), "gy", [GY_ORDER])
    back = x_back(mixed, x_inverse)
    back = exchange(back.reshape(GX, ROWS, 128), "gx").reshape(GX * ROWS, 128)
    out = final_stage(field, back, depth_table(), bypass_weight, bypass_bias)
    return out.reshape(1, C, RX, RY, ZT)


def solution(mesh):
    in_specs = (P(None, None, "gx", "gy", None), P(None, None, None, ("gx", "gy")), P(), P())
    out_specs = P(None, None, "gx", "gy", None)
    return jax.shard_map(shards, mesh=mesh, in_specs=in_specs, out_specs=out_specs, check_vma=False)
```

```python
import math

import jax
import jax.numpy as jnp
import ml_dtypes
import numpy as np
from jax import lax
from jax.experimental import pallas as pl
from jax.experimental.pallas import tpu as pltpu
from jax.sharding import PartitionSpec as P

C, NX, NY, NZ, NT = 20, 128, 128, 32, 24
KX, KY, KZ, KT = 24, 24, 16, 12
ZT, MZT = NZ * NT, KZ * KT
GX = GY = 16
RX, RY = NX // GX, NY // GY
BM = MZT // GX
H = BM * KX // GY
HQ = 2 * H
CM, CR = 16, 4
MAIN = BM * 2 * RX
ROWS = MAIN + BM * 2 * RX * CR // CM
HALF = ZT // 2
LANES = 768
MIB = 1024 * 1024

NN = (((1,), (0,)), ((), ()))
NT_DIMS = (((1,), (1,)), ((), ()))


GY_ORDER = [x * 4 + z for z in (0, 2, 1, 3) for x in (0, 2, 1, 3)]


def slot_mode(slot):
    return (slot % 4) * 3 + slot // 4


def kept(count, length):
    steps = np.arange(count)
    return np.where(steps < count // 2, steps, length - count + steps)


def halves(table):
    table = table.astype(np.float32)
    high = table.astype(ml_dtypes.bfloat16)
    low = (table - high.astype(np.float32)).astype(ml_dtypes.bfloat16)
    return np.stack([high, low])


def depth_table():
    kz = kept(KZ, NZ)
    modes = np.array([g * BM + slot_mode(s) for g in range(GX) for s in range(BM)])
    z_freq, t_freq = kz[modes // KT], modes % KT
    cells = np.arange(ZT)
    turns = (z_freq[:, None] * (cells // NT)[None] * NT + t_freq[:, None] * (cells % NT)[None] * NZ) % ZT
    angle = turns * (2.0 * np.pi / ZT)
    cosine, sine = np.cos(angle), np.sin(angle)
    scale = (np.where(t_freq == 0, 1.0, 2.0) / (NX * NY * ZT))[:, None]
    inverse = np.stack([cosine * scale, -sine * scale], axis=1).reshape(2 * MZT, ZT)
    return right_table(inverse)


def x_tables():
    angle = (np.arange(NX)[:, None] * kept(KX, NX)[None] % NX) * (2.0 * np.pi / NX)
    cosine, sine = np.cos(angle), np.sin(angle)
    forward = np.stack([np.stack([cosine, -sine], -1), np.stack([sine, cosine], -1)], 1)
    back = np.stack([np.stack([cosine, -sine], -1), np.stack([sine, cosine], -1)], 1)
    shape = (GX, RX, 2, KX * 2)
    forward, back = forward.reshape(shape), back.reshape(shape)
    def main(table):
        return table.transpose(0, 2, 1, 3).reshape(GX * 2 * RX, KX * 2)
    def rest(table):
        return table.reshape(GX * RX * 2, KX * 2)
    return (
        np.stack([left_table(main(forward).T), left_table(rest(forward).T)]),
        np.stack([left_table(main(back)), left_table(rest(back))]),
    )


def y_tables():
    angle = (np.arange(NY)[:, None] * kept(KY, NY)[None] % NY) * (2.0 * np.pi / NY)
    cosine, sine = np.cos(angle), np.sin(angle)
    both = np.concatenate([cosine, sine], axis=1)
    both = both.reshape(GY, RY, 2 * KY)[np.array(GY_ORDER)].reshape(NY, 2 * KY)
    return left_table(both.T), left_table(both)


def split(value):
    high = value.astype(jnp.bfloat16)
    return high, (value - high.astype(jnp.float32)).astype(jnp.bfloat16)


def stacked_left(value, axis):
    high, low = split(value)
    return jnp.concatenate([high, high, low], axis=axis)


def stacked_right(value, axis):
    high, low = split(value)
    return jnp.concatenate([high, low, high], axis=axis)


def left_table(table):
    high, low = halves(table)
    return np.concatenate([high, high, low], axis=1)


def right_table(table):
    high, low = halves(table)
    return np.concatenate([high, low, high], axis=0)


def dot(left, right, dims):
    return lax.dot_general(left, right, dims, preferred_element_type=jnp.float32)


def block_swap(value):
    row = lax.broadcasted_iota(jnp.int32, value.shape, 1) // 2
    lane = lax.broadcasted_iota(jnp.int32, value.shape, 2) // 32
    far = pltpu.roll(pltpu.roll(value, 4, 1), 64, 2)
    value = jnp.where((row // 2) == (lane // 2), value, far)
    up = pltpu.roll(pltpu.roll(value, 6, 1), 32, 2)
    down = pltpu.roll(pltpu.roll(value, 2, 1), 96, 2)
    return jnp.where((row % 2) == (lane % 2), value, jnp.where(row % 2 == 0, up, down))


def divide(value, by):
    return (value * 2731) >> 16 if by == 24 else value // by


def cos_sin(index, length):
    half = (index - length // 2).astype(jnp.float32) * np.float32(np.pi / length)
    square = half * half
    sine, cosine = jnp.zeros_like(half), jnp.zeros_like(half)
    for power in range(14, -1, -2):
        sign = -1.0 if power % 4 else 1.0
        cosine = cosine * square + np.float32(sign / math.factorial(power))
        sine = sine * square + np.float32(sign / math.factorial(power + 1))
    sine = sine * half
    return 2.0 * sine * sine - 1.0, -2.0 * sine * cosine


def fill_forward_table(table):
    def cells(rows):
        row = lax.broadcasted_iota(jnp.int32, (rows, HALF), 0)
        lane = lax.broadcasted_iota(jnp.int32, (rows, HALF), 1)
        z = divide(lane, NT)
        return row, z, lane - NT * z
    row, z, _ = cells(GX)
    z_freq = jnp.where(row < KZ // 2, row, row + NZ - KZ)
    z_cos, z_sin = cos_sin((z_freq * z) % NZ, NZ)
    row, _, t = cells(2 * BM)
    slot = row >> 1
    turns = ((slot & 3) * 3 + (slot >> 2)) * t
    t_cos, t_sin = cos_sin(turns - NT * divide(turns, NT), NT)
    real = (row & 1) == 0
    one = jnp.where(real, t_cos, -t_sin)
    two = jnp.where(real, -t_sin, -t_cos)
    for odd in range(2):
        rows = [z_cos[g : g + 1] * one + z_sin[g : g + 1] * two for g in range(odd, GX, 2)]
        table[odd] = jnp.concatenate(split(jnp.concatenate(rows, axis=0)), axis=0)


def depth_modes(cells, table):
    near, far = cells[:, :HALF], cells[:, HALF:]
    modes = []
    for odd in range(2):
        high, low = split(near - far if odd else near + far)
        both = dot(table[odd], high, NT_DIMS)
        modes.append(both[:MZT] + (both[MZT:] + dot(table[odd, :MZT], low, NT_DIMS)))
    return modes


def depth_kernel(field, out, held, table, arrived):
    copies = [
        pltpu.make_async_copy(field.at[:, pl.ds(2 * pair, 2)], held.at[pair], arrived.at[pair])
        for pair in range(4)
    ]
    for copy in copies:
        copy.start()
    fill_forward_table(table)
    for pair in range(4):
        if pair < 2:
            for copy in copies[pair : 1 + 3 * pair]:
                copy.wait()
        cells = jnp.concatenate(
            [held[pair, 0:CM, k].reshape(CM * RY, ZT) for k in range(2)], axis=0
        )
        modes = depth_modes(cells, table)
        for k in range(2):
            for dest in range(GX):
                start = dest * ROWS + 2 * pair + k
                row = dest // 2 * 2 * BM
                out[pl.ds(start, 2 * BM, stride=RX), :] = modes[dest % 2][
                    row : row + 2 * BM, k * 128 : (k + 1) * 128
                ]
    cells = jnp.concatenate(
        [held[k // 2, CM:C, k % 2].reshape(CR * RY, ZT) for k in range(RX)], axis=0
    )
    modes = depth_modes(cells, table)
    for half in range(2):
        for odd in range(2):
            tiles = block_swap(modes[odd][:, half * 128 : (half + 1) * 128].reshape(GX // 2 * 3, 8, 128))
            for dest in range(odd, GX, 2):
                for third in range(3):
                    start = dest * ROWS + MAIN + third * 16 + half * 8
                    out[pl.ds(start, 8), :] = tiles[dest // 2 * 3 + third]


def depth_transform(field):
    return pl.pallas_call(
        depth_kernel,
        in_specs=[pl.BlockSpec(memory_space=pltpu.HBM)],
        out_shape=jax.ShapeDtypeStruct((GX * ROWS, 128), jnp.float32),
        scratch_shapes=[
            pltpu.VMEM((4, C, 2, RY, ZT), jnp.float32),
            pltpu.VMEM((2, 2 * MZT, HALF), jnp.bfloat16),
            pltpu.SemaphoreType.DMA((4,)),
        ],
        compiler_params=pltpu.CompilerParams(vmem_limit_bytes=50 * MIB),
        cost_estimate=pl.CostEstimate(flops=1200000000, bytes_accessed=6000000, transcendentals=0),
        name="depth_forward",
    )(field)


def x_kernel(cells, table, out, held):
    main_table, rest_table = table[0], table[1]
    for slot in range(BM):
        columns = jnp.concatenate(
            [cells[pl.ds(s * ROWS + slot * 16, 16), :] for s in range(GX)], axis=0
        )
        mode = slot_mode(slot)
        held[pl.ds(mode * 2 * KX, 2 * KX), :] = dot(main_table, stacked_right(columns, 0), NN)
    for third in range(3):
        columns = jnp.concatenate(
            [cells[pl.ds(s * ROWS + MAIN + third * 16, 16), :] for s in range(GX)], axis=0
        )
        held[pl.ds((BM + third) * 2 * KX, 2 * KX), :] = dot(rest_table, stacked_right(columns, 0), NN)
    for g in range(GY):
        place = GY_ORDER.index(g)
        turned = held[pl.ds(g * HQ, HQ), :].T
        for c in range(CM):
            out[place, :, c * HQ : (c + 1) * HQ] = turned[c * RY : (c + 1) * RY]
    for b in range(4):
        turned = held[pl.ds(BM * 2 * KX + b * HQ, HQ), :].T
        for a in range(4):
            for c in range(CR):
                row = (a * CR + c) * RY
                out[GY_ORDER.index(4 * a + b), :, (CM + c) * HQ : (CM + c + 1) * HQ] = turned[row : row + RY]
    for g in range(GY):
        out[g, :, C * HQ : LANES] = jnp.zeros((RY, LANES - C * HQ), jnp.float32)


def x_transform(cells, table):
    return pl.pallas_call(
        x_kernel,
        out_shape=jax.ShapeDtypeStruct((GY, RY, LANES), jnp.float32),
        scratch_shapes=[pltpu.VMEM(((BM + 3) * 2 * KX, 128), jnp.float32)],
        compiler_params=pltpu.CompilerParams(vmem_limit_bytes=40 * MIB),
        cost_estimate=pl.CostEstimate(flops=150000000, bytes_accessed=2500000, transcendentals=0),
        name="x_forward",
    )(cells, table)


def even_lanes(shape):
    return lax.broadcasted_iota(jnp.int32, shape, len(shape) - 1) % 2 == 0


def turn_parts(value, even):
    lanes = value.shape[-1]
    return jnp.where(even, -pltpu.roll(value, lanes - 1, 1), pltpu.roll(value, 1, 1))


def mix_kernel(cells, weights, forward, back, out, reals, imags, mixed):
    sums = dot(forward[...], stacked_right(cells[...].reshape(GY * RY, LANES), 0), NN)
    even = even_lanes((KY, LANES))
    coef = sums[:KY] - turn_parts(sums[KY:], even)
    real = jnp.where(even, coef, pltpu.roll(coef, 1, 1))
    imag = jnp.where(even, pltpu.roll(coef, LANES - 1, 1), coef)
    for i in range(C):
        reals[i] = real[:, i * HQ : (i + 1) * HQ]
        imags[i] = imag[:, i * HQ : (i + 1) * HQ]
    even_pairs = even_lanes((KY, HQ))
    group = 4
    for first in range(0, C, group):
        one = [jnp.zeros((KY, HQ), jnp.float32)] * group
        two = [jnp.zeros((KY, HQ), jnp.float32)] * group
        for i in range(C):
            real_i, imag_i = reals[i], imags[i]
            for k in range(group):
                weight = weights[i, first + k]
                one[k] = one[k] + weight * real_i
                two[k] = two[k] + weight * imag_i
        for k in range(group):
            o = first + k
            mixed[:, o * HQ : (o + 1) * HQ] = one[k] + turn_parts(two[k], even_pairs)
    mixed[:, C * HQ : LANES] = jnp.zeros((KY, LANES - C * HQ), jnp.float32)
    modes = mixed[...]
    both = jnp.concatenate([modes, turn_parts(modes, even)], axis=0)
    out[...] = dot(back[...], stacked_right(both, 0), NN).reshape(GY, RY, LANES)


def mix_modes(cells, weights, forward, back):
    return pl.pallas_call(
        mix_kernel,
        out_shape=jax.ShapeDtypeStruct((GY, RY, LANES), jnp.float32),
        scratch_shapes=[
            pltpu.VMEM((C, KY, HQ), jnp.float32),
            pltpu.VMEM((C, KY, HQ), jnp.float32),
            pltpu.VMEM((KY, LANES), jnp.float32),
        ],
        compiler_params=pltpu.CompilerParams(vmem_limit_bytes=40 * MIB),
        cost_estimate=pl.CostEstimate(flops=60000000, bytes_accessed=6000000, transcendentals=0),
        name="y_mix",
    )(cells, weights, forward, back)


def x_back_kernel(modes, table, out, held):
    main_table, rest_table = table[0], table[1]
    for g in range(GY):
        place = GY_ORDER.index(g)
        rows = jnp.concatenate([modes[place, :, c * HQ : (c + 1) * HQ] for c in range(CM)], axis=0)
        held[pl.ds(g * HQ, HQ), :] = rows.T
    for b in range(4):
        rows = jnp.concatenate(
            [
                modes[GY_ORDER.index(4 * a + b), :, (CM + c) * HQ : (CM + c + 1) * HQ]
                for a in range(4)
                for c in range(CR)
            ],
            axis=0,
        )
        held[pl.ds(BM * 2 * KX + b * HQ, HQ), :] = rows.T
    for slot in range(BM):
        mode = slot_mode(slot)
        columns = held[pl.ds(mode * 2 * KX, 2 * KX), :]
        cells = dot(main_table, stacked_right(columns, 0), NN)
        for s in range(GX):
            out[pl.ds(s * ROWS + slot * 16, 16), :] = cells[s * 16 : (s + 1) * 16]
    for third in range(3):
        columns = held[pl.ds((BM + third) * 2 * KX, 2 * KX), :]
        cells = dot(rest_table, stacked_right(columns, 0), NN)
        for s in range(GX):
            out[pl.ds(s * ROWS + MAIN + third * 16, 16), :] = cells[s * 16 : (s + 1) * 16]


def x_back(modes, table):
    return pl.pallas_call(
        x_back_kernel,
        out_shape=jax.ShapeDtypeStruct((GX * ROWS, 128), jnp.float32),
        scratch_shapes=[pltpu.VMEM(((BM + 3) * 2 * KX, 128), jnp.float32)],
        compiler_params=pltpu.CompilerParams(vmem_limit_bytes=40 * MIB),
        cost_estimate=pl.CostEstimate(flops=150000000, bytes_accessed=2500000, transcendentals=0),
        name="x_back",
    )(modes, table)


def spread_map(channel_map):
    rows = C * RY
    copy = lax.broadcasted_iota(jnp.int32, (C, rows), 1) // RY
    copy = (copy == lax.broadcasted_iota(jnp.int32, (C, rows), 0)).astype(jnp.bfloat16)
    same = lax.broadcasted_iota(jnp.int32, (rows, rows), 0) % RY
    same = same == lax.broadcasted_iota(jnp.int32, (rows, rows), 1) % RY
    spread = []
    for half in split(channel_map):
        wide = lax.dot_general(half, copy, NN, preferred_element_type=jnp.float32)
        tall = jnp.broadcast_to(wide[:, None], (C, RY, rows)).reshape(rows, rows)
        spread.append(jnp.where(same, tall, 0.0).astype(jnp.bfloat16))
    return spread


def final_kernel(field, cells, table, channel_map, bias, out, held, left):
    high, low = spread_map(channel_map[...])
    spread = jnp.concatenate([high, high, low], axis=1)
    copies = []
    for pair in range(RX // 2):
        if pair % 2 == 0:
            tiles = jnp.stack(
                [
                    cells[pl.ds(s * ROWS + MAIN + third * 16 + (pair // 2) * 8, 8), :]
                    for s in range(GX)
                    for third in range(3)
                ]
            )
            rest = block_swap(tiles).reshape(2 * MZT, 128).T
        columns = []
        for k in range(2):
            main = jnp.concatenate(
                [cells[pl.ds(s * ROWS + 2 * pair + k, 2 * BM, stride=RX), :] for s in range(GX)],
                axis=0,
            )
            row = ((pair % 2) * 2 + k) * CR * RY
            columns += [main.T, rest[row : row + CR * RY]]
        spectral = dot(stacked_left(jnp.concatenate(columns, axis=0), 1), table[...], NN)
        for k in range(2):
            x = 2 * pair + k
            bypass = dot(spread, stacked_right(field[:, x].reshape(C * RY, ZT), 0), NN)
            value = spectral[k * C * RY : (k + 1) * C * RY] + bypass
            for c in range(C):
                one = value[c * RY : (c + 1) * RY] + bias[c]
                held[c, x] = 0.5 * one * (1.0 + lax.erf(one * np.float32(np.sqrt(0.5))))
            copies.append(pltpu.make_async_copy(held.at[:, x], out.at[:, x], left.at[x]))
            copies[-1].start()
    for copy in copies:
        copy.wait()


def final_stage(field, cells, table, channel_map, bias):
    whole = pl.BlockSpec(memory_space=pltpu.VMEM)
    return pl.pallas_call(
        final_kernel,
        in_specs=[whole, whole, whole, whole, pl.BlockSpec(memory_space=pltpu.SMEM)],
        out_specs=pl.BlockSpec(memory_space=pltpu.HBM),
        out_shape=jax.ShapeDtypeStruct((C, RX, RY, ZT), jnp.float32),
        scratch_shapes=[
            pltpu.VMEM((C, RX, RY, ZT), jnp.float32),
            pltpu.SemaphoreType.DMA((RX,)),
        ],
        compiler_params=pltpu.CompilerParams(vmem_limit_bytes=40 * MIB),
        cost_estimate=pl.CostEstimate(flops=3200000000, bytes_accessed=11000000, transcendentals=1000000),
        name="depth_back",
    )(field, cells, table, channel_map, bias)


def exchange(value, axis, groups=None):
    return lax.all_to_all(
        value, axis, split_axis=0, concat_axis=0, axis_index_groups=groups, tiled=True
    )


def shards(field, spec_weight, bypass_weight, bypass_bias):
    x_forward, x_inverse = x_tables()
    y_forward, y_inverse = y_tables()
    field = field.reshape(C, RX, RY, ZT)
    modes = depth_transform(field)
    cells = exchange(modes.reshape(GX, ROWS, 128), "gx").reshape(GX * ROWS, 128)
    pairs = exchange(x_transform(cells, x_forward), "gy", [GY_ORDER])
    mixed = exchange(mix_modes(pairs, spec_weight, y_forward, y_inverse), "gy", [GY_ORDER])
    back = x_back(mixed, x_inverse)
    back = exchange(back.reshape(GX, ROWS, 128), "gx").reshape(GX * ROWS, 128)
    out = final_stage(field, back, depth_table(), bypass_weight, bypass_bias)
    return out.reshape(1, C, RX, RY, ZT)


def solution(mesh):
    in_specs = (P(None, None, "gx", "gy", None), P(None, None, None, ("gx", "gy")), P(), P())
    out_specs = P(None, None, "gx", "gy", None)
    return jax.shard_map(shards, mesh=mesh, in_specs=in_specs, out_specs=out_specs, check_vma=False)
```

```python
import math

import jax
import jax.numpy as jnp
import ml_dtypes
import numpy as np
from jax import lax
from jax.experimental import pallas as pl
from jax.experimental.pallas import tpu as pltpu
from jax.sharding import PartitionSpec as P

C, NX, NY, NZ, NT = 20, 128, 128, 32, 24
KX, KY, KZ, KT = 24, 24, 16, 12
ZT, MZT = NZ * NT, KZ * KT
GX = GY = 16
RX, RY = NX // GX, NY // GY
BM = MZT // GX
H = BM * KX // GY
HQ = 2 * H
CM, CR = 16, 4
MAIN = BM * 2 * RX
ROWS = MAIN + BM * 2 * RX * CR // CM
HALF = ZT // 2
LANES = 768
MIB = 1024 * 1024

NN = (((1,), (0,)), ((), ()))
NT_DIMS = (((1,), (1,)), ((), ()))


GY_ORDER = [x * 4 + z for z in range(4) for x in range(4)]


def slot_mode(slot):
    return (slot % 4) * 3 + slot // 4


def kept(count, length):
    steps = np.arange(count)
    return np.where(steps < count // 2, steps, length - count + steps)


def halves(table):
    table = table.astype(np.float32)
    high = table.astype(ml_dtypes.bfloat16)
    low = (table - high.astype(np.float32)).astype(ml_dtypes.bfloat16)
    return np.stack([high, low])


def depth_table():
    kz = kept(KZ, NZ)
    modes = np.array([g * BM + slot_mode(s) for g in range(GX) for s in range(BM)])
    z_freq, t_freq = kz[modes // KT], modes % KT
    cells = np.arange(ZT)
    turns = (z_freq[:, None] * (cells // NT)[None] * NT + t_freq[:, None] * (cells % NT)[None] * NZ) % ZT
    angle = turns * (2.0 * np.pi / ZT)
    cosine, sine = np.cos(angle), np.sin(angle)
    scale = (np.where(t_freq == 0, 1.0, 2.0) / (NX * NY * ZT))[:, None]
    inverse = np.stack([cosine * scale, -sine * scale], axis=1).reshape(2 * MZT, ZT)
    return right_table(inverse)


def x_tables():
    angle = (np.arange(NX)[:, None] * kept(KX, NX)[None] % NX) * (2.0 * np.pi / NX)
    cosine, sine = np.cos(angle), np.sin(angle)
    forward = np.stack([np.stack([cosine, -sine], -1), np.stack([sine, cosine], -1)], 1)
    back = np.stack([np.stack([cosine, -sine], -1), np.stack([sine, cosine], -1)], 1)
    shape = (GX, RX, 2, KX * 2)
    forward, back = forward.reshape(shape), back.reshape(shape)
    def main(table):
        return table.transpose(0, 2, 1, 3).reshape(GX * 2 * RX, KX * 2)
    def rest(table):
        return table.reshape(GX * RX * 2, KX * 2)
    return (
        np.stack([left_table(main(forward).T), left_table(rest(forward).T)]),
        np.stack([left_table(main(back)), left_table(rest(back))]),
    )


def y_tables():
    angle = (np.arange(NY)[:, None] * kept(KY, NY)[None] % NY) * (2.0 * np.pi / NY)
    cosine, sine = np.cos(angle), np.sin(angle)
    both = np.concatenate([cosine, sine], axis=1)
    both = both.reshape(GY, RY, 2 * KY)[np.array(GY_ORDER)].reshape(NY, 2 * KY)
    return left_table(both.T), left_table(both)


def split(value):
    high = value.astype(jnp.bfloat16)
    return high, (value - high.astype(jnp.float32)).astype(jnp.bfloat16)


def stacked_left(value, axis):
    high, low = split(value)
    return jnp.concatenate([high, high, low], axis=axis)


def stacked_right(value, axis):
    high, low = split(value)
    return jnp.concatenate([high, low, high], axis=axis)


def left_table(table):
    high, low = halves(table)
    return np.concatenate([high, high, low], axis=1)


def right_table(table):
    high, low = halves(table)
    return np.concatenate([high, low, high], axis=0)


def dot(left, right, dims):
    return lax.dot_general(left, right, dims, preferred_element_type=jnp.float32)


def block_swap(value):
    row = lax.broadcasted_iota(jnp.int32, value.shape, 1) // 2
    lane = lax.broadcasted_iota(jnp.int32, value.shape, 2) // 32
    far = pltpu.roll(pltpu.roll(value, 4, 1), 64, 2)
    value = jnp.where((row // 2) == (lane // 2), value, far)
    up = pltpu.roll(pltpu.roll(value, 6, 1), 32, 2)
    down = pltpu.roll(pltpu.roll(value, 2, 1), 96, 2)
    return jnp.where((row % 2) == (lane % 2), value, jnp.where(row % 2 == 0, up, down))


def divide(value, by):
    return (value * 2731) >> 16 if by == 24 else value // by


def cos_sin(index, length):
    half = (index - length // 2).astype(jnp.float32) * np.float32(np.pi / length)
    square = half * half
    sine, cosine = jnp.zeros_like(half), jnp.zeros_like(half)
    for power in range(14, -1, -2):
        sign = -1.0 if power % 4 else 1.0
        cosine = cosine * square + np.float32(sign / math.factorial(power))
        sine = sine * square + np.float32(sign / math.factorial(power + 1))
    sine = sine * half
    return 2.0 * sine * sine - 1.0, -2.0 * sine * cosine


def fill_forward_table(table):
    def cells(rows):
        row = lax.broadcasted_iota(jnp.int32, (rows, HALF), 0)
        lane = lax.broadcasted_iota(jnp.int32, (rows, HALF), 1)
        z = divide(lane, NT)
        return row, z, lane - NT * z
    row, z, _ = cells(GX)
    z_freq = jnp.where(row < KZ // 2, row, row + NZ - KZ)
    z_cos, z_sin = cos_sin((z_freq * z) % NZ, NZ)
    row, _, t = cells(2 * BM)
    slot = row >> 1
    turns = ((slot & 3) * 3 + (slot >> 2)) * t
    t_cos, t_sin = cos_sin(turns - NT * divide(turns, NT), NT)
    real = (row & 1) == 0
    one = jnp.where(real, t_cos, -t_sin)
    two = jnp.where(real, -t_sin, -t_cos)
    for odd in range(2):
        rows = [z_cos[g : g + 1] * one + z_sin[g : g + 1] * two for g in range(odd, GX, 2)]
        table[odd] = jnp.concatenate(split(jnp.concatenate(rows, axis=0)), axis=0)


def depth_modes(cells, table):
    near, far = cells[:, :HALF], cells[:, HALF:]
    modes = []
    for odd in range(2):
        high, low = split(near - far if odd else near + far)
        both = dot(table[odd], high, NT_DIMS)
        modes.append(both[:MZT] + (both[MZT:] + dot(table[odd, :MZT], low, NT_DIMS)))
    return modes


def depth_kernel(field, out, held, table, arrived):
    copies = [
        pltpu.make_async_copy(field.at[:, pl.ds(2 * pair, 2)], held.at[pair], arrived.at[pair])
        for pair in range(4)
    ]
    for copy in copies:
        copy.start()
    fill_forward_table(table)
    for pair in range(4):
        if pair < 2:
            for copy in copies[pair : 1 + 3 * pair]:
                copy.wait()
        cells = jnp.concatenate(
            [held[pair, 0:CM, k].reshape(CM * RY, ZT) for k in range(2)], axis=0
        )
        modes = depth_modes(cells, table)
        for k in range(2):
            for dest in range(GX):
                start = dest * ROWS + 2 * pair + k
                row = dest // 2 * 2 * BM
                out[pl.ds(start, 2 * BM, stride=RX), :] = modes[dest % 2][
                    row : row + 2 * BM, k * 128 : (k + 1) * 128
                ]
    cells = jnp.concatenate(
        [held[k // 2, CM:C, k % 2].reshape(CR * RY, ZT) for k in range(RX)], axis=0
    )
    modes = depth_modes(cells, table)
    for half in range(2):
        for odd in range(2):
            tiles = block_swap(modes[odd][:, half * 128 : (half + 1) * 128].reshape(GX // 2 * 3, 8, 128))
            for dest in range(odd, GX, 2):
                for third in range(3):
                    start = dest * ROWS + MAIN + third * 16 + half * 8
                    out[pl.ds(start, 8), :] = tiles[dest // 2 * 3 + third]


def depth_transform(field):
    return pl.pallas_call(
        depth_kernel,
        in_specs=[pl.BlockSpec(memory_space=pltpu.HBM)],
        out_shape=jax.ShapeDtypeStruct((GX * ROWS, 128), jnp.float32),
        scratch_shapes=[
            pltpu.VMEM((4, C, 2, RY, ZT), jnp.float32),
            pltpu.VMEM((2, 2 * MZT, HALF), jnp.bfloat16),
            pltpu.SemaphoreType.DMA((4,)),
        ],
        compiler_params=pltpu.CompilerParams(vmem_limit_bytes=50 * MIB),
        cost_estimate=pl.CostEstimate(flops=1200000000, bytes_accessed=6000000, transcendentals=0),
        name="depth_forward",
    )(field)


def x_kernel(cells, table, out):
    def modes_of(first, which):
        columns = jnp.concatenate(
            [cells[pl.ds(s * ROWS + first, 16), :] for s in range(GX)], axis=0
        )
        return dot(table[which], stacked_right(columns, 0), NN)

    slots = [0] * BM
    for slot in range(BM):
        slots[slot_mode(slot)] = slot
    for a in range(4):
        modes = jnp.concatenate([modes_of(slots[3 * a + m] * 16, 0) for m in range(3)], axis=0)
        for b in range(4):
            place = GY_ORDER.index(4 * a + b)
            turned = modes[b * HQ : (b + 1) * HQ].T
            for c in range(CM):
                out[place, :, c * HQ : (c + 1) * HQ] = turned[c * RY : (c + 1) * RY]
    modes = jnp.concatenate([modes_of(MAIN + m * 16, 1) for m in range(3)], axis=0)
    for b in range(4):
        turned = modes[b * HQ : (b + 1) * HQ].T
        for a in range(4):
            place = GY_ORDER.index(4 * a + b)
            for c in range(CR):
                row = (a * CR + c) * RY
                out[place, :, (CM + c) * HQ : (CM + c + 1) * HQ] = turned[row : row + RY]
            out[place, :, C * HQ : LANES] = jnp.zeros((RY, LANES - C * HQ), jnp.float32)


def x_transform(cells, table):
    return pl.pallas_call(
        x_kernel,
        out_shape=jax.ShapeDtypeStruct((GY, RY, LANES), jnp.float32),
        compiler_params=pltpu.CompilerParams(vmem_limit_bytes=40 * MIB),
        cost_estimate=pl.CostEstimate(flops=150000000, bytes_accessed=2500000, transcendentals=0),
        name="x_forward",
    )(cells, table)


def even_lanes(shape):
    return lax.broadcasted_iota(jnp.int32, shape, len(shape) - 1) % 2 == 0


def turn_parts(value, even):
    lanes = value.shape[-1]
    return jnp.where(even, -pltpu.roll(value, lanes - 1, 1), pltpu.roll(value, 1, 1))


def mix_kernel(cells, weights, forward, back, out, reals, imags, mixed):
    sums = dot(forward[...], stacked_right(cells[...].reshape(GY * RY, LANES), 0), NN)
    even = even_lanes((KY, LANES))
    coef = sums[:KY] - turn_parts(sums[KY:], even)
    real = jnp.where(even, coef, pltpu.roll(coef, 1, 1))
    imag = jnp.where(even, pltpu.roll(coef, LANES - 1, 1), coef)
    for i in range(C):
        reals[i] = real[:, i * HQ : (i + 1) * HQ]
        imags[i] = imag[:, i * HQ : (i + 1) * HQ]
    even_pairs = even_lanes((KY, HQ))
    group = 10
    for first in range(0, C, group):
        one = [jnp.zeros((KY, HQ), jnp.float32)] * group
        two = [jnp.zeros((KY, HQ), jnp.float32)] * group
        for i in range(C):
            real_i, imag_i = reals[i], imags[i]
            for k in range(group):
                weight = weights[i, first + k]
                one[k] = one[k] + weight * real_i
                two[k] = two[k] + weight * imag_i
        for k in range(group):
            o = first + k
            mixed[:, o * HQ : (o + 1) * HQ] = one[k] + turn_parts(two[k], even_pairs)
    mixed[:, C * HQ : LANES] = jnp.zeros((KY, LANES - C * HQ), jnp.float32)
    modes = mixed[...]
    both = jnp.concatenate([modes, turn_parts(modes, even)], axis=0)
    out[...] = dot(back[...], stacked_right(both, 0), NN).reshape(GY, RY, LANES)


def mix_modes(cells, weights, forward, back):
    return pl.pallas_call(
        mix_kernel,
        out_shape=jax.ShapeDtypeStruct((GY, RY, LANES), jnp.float32),
        scratch_shapes=[
            pltpu.VMEM((C, KY, HQ), jnp.float32),
            pltpu.VMEM((C, KY, HQ), jnp.float32),
            pltpu.VMEM((KY, LANES), jnp.float32),
        ],
        compiler_params=pltpu.CompilerParams(vmem_limit_bytes=40 * MIB),
        cost_estimate=pl.CostEstimate(flops=60000000, bytes_accessed=6000000, transcendentals=0),
        name="y_mix",
    )(cells, weights, forward, back)


def x_back_kernel(modes, table, out):
    def write(first, which, columns):
        cells = dot(table[which], stacked_right(columns, 0), NN)
        for s in range(GX):
            out[pl.ds(s * ROWS + first, 16), :] = cells[s * 16 : (s + 1) * 16]

    def columns_of(pieces):
        rows = jnp.concatenate(
            [modes[GY_ORDER.index(g), :, c * HQ : (c + 1) * HQ] for g, c in pieces], axis=0
        )
        return rows.T

    slots = [0] * BM
    for slot in range(BM):
        slots[slot_mode(slot)] = slot
    for a in range(4):
        parts = [columns_of([(4 * a + b, c) for c in range(CM)]) for b in range(4)]
        columns = jnp.concatenate(parts, axis=0)
        for m in range(3):
            write(slots[3 * a + m] * 16, 0, columns[m * 2 * KX : (m + 1) * 2 * KX])
    parts = [
        columns_of([(4 * a + b, CM + c) for a in range(4) for c in range(CR)]) for b in range(4)
    ]
    columns = jnp.concatenate(parts, axis=0)
    for m in range(3):
        write(MAIN + m * 16, 1, columns[m * 2 * KX : (m + 1) * 2 * KX])


def x_back(modes, table):
    return pl.pallas_call(
        x_back_kernel,
        out_shape=jax.ShapeDtypeStruct((GX * ROWS, 128), jnp.float32),
        compiler_params=pltpu.CompilerParams(vmem_limit_bytes=40 * MIB),
        cost_estimate=pl.CostEstimate(flops=150000000, bytes_accessed=2500000, transcendentals=0),
        name="x_back",
    )(modes, table)


def spread_map(channel_map):
    rows = C * RY
    copy = lax.broadcasted_iota(jnp.int32, (C, rows), 1) // RY
    copy = (copy == lax.broadcasted_iota(jnp.int32, (C, rows), 0)).astype(jnp.bfloat16)
    same = lax.broadcasted_iota(jnp.int32, (rows, rows), 0) % RY
    same = same == lax.broadcasted_iota(jnp.int32, (rows, rows), 1) % RY
    spread = []
    for half in split(channel_map):
        wide = lax.dot_general(half, copy, NN, preferred_element_type=jnp.float32)
        tall = jnp.broadcast_to(wide[:, None], (C, RY, rows)).reshape(rows, rows)
        spread.append(jnp.where(same, tall, 0.0).astype(jnp.bfloat16))
    return spread


def final_kernel(field, cells, table, channel_map, bias, out, held, left):
    high, low = spread_map(channel_map[...])
    spread = jnp.concatenate([high, high, low], axis=1)
    copies = []
    for pair in range(RX // 2):
        if pair % 2 == 0:
            tiles = jnp.stack(
                [
                    cells[pl.ds(s * ROWS + MAIN + third * 16 + (pair // 2) * 8, 8), :]
                    for s in range(GX)
                    for third in range(3)
                ]
            )
            rest = block_swap(tiles).reshape(2 * MZT, 128).T
        columns = []
        for k in range(2):
            main = jnp.concatenate(
                [cells[pl.ds(s * ROWS + 2 * pair + k, 2 * BM, stride=RX), :] for s in range(GX)],
                axis=0,
            )
            row = ((pair % 2) * 2 + k) * CR * RY
            columns += [main.T, rest[row : row + CR * RY]]
        spectral = dot(stacked_left(jnp.concatenate(columns, axis=0), 1), table[...], NN)
        for k in range(2):
            x = 2 * pair + k
            bypass = dot(spread, stacked_right(field[:, x].reshape(C * RY, ZT), 0), NN)
            value = spectral[k * C * RY : (k + 1) * C * RY] + bypass
            for c in range(C):
                one = value[c * RY : (c + 1) * RY] + bias[c]
                held[c, x] = 0.5 * one * (1.0 + lax.erf(one * np.float32(np.sqrt(0.5))))
            copies.append(pltpu.make_async_copy(held.at[:, x], out.at[:, x], left.at[x]))
            copies[-1].start()
    for copy in copies:
        copy.wait()


def final_stage(field, cells, table, channel_map, bias):
    whole = pl.BlockSpec(memory_space=pltpu.VMEM)
    return pl.pallas_call(
        final_kernel,
        in_specs=[whole, whole, whole, whole, pl.BlockSpec(memory_space=pltpu.SMEM)],
        out_specs=pl.BlockSpec(memory_space=pltpu.HBM),
        out_shape=jax.ShapeDtypeStruct((C, RX, RY, ZT), jnp.float32),
        scratch_shapes=[
            pltpu.VMEM((C, RX, RY, ZT), jnp.float32),
            pltpu.SemaphoreType.DMA((RX,)),
        ],
        compiler_params=pltpu.CompilerParams(vmem_limit_bytes=40 * MIB),
        cost_estimate=pl.CostEstimate(flops=3200000000, bytes_accessed=11000000, transcendentals=1000000),
        name="depth_back",
    )(field, cells, table, channel_map, bias)


def exchange(value, axis, groups=None):
    return lax.all_to_all(
        value, axis, split_axis=0, concat_axis=0, axis_index_groups=groups, tiled=True
    )


def shards(field, spec_weight, bypass_weight, bypass_bias):
    x_forward, x_inverse = x_tables()
    y_forward, y_inverse = y_tables()
    field = field.reshape(C, RX, RY, ZT)
    modes = depth_transform(field)
    cells = exchange(modes.reshape(GX, ROWS, 128), "gx").reshape(GX * ROWS, 128)
    pairs = exchange(x_transform(cells, x_forward), "gy", [GY_ORDER])
    mixed = exchange(mix_modes(pairs, spec_weight, y_forward, y_inverse), "gy", [GY_ORDER])
    back = x_back(mixed, x_inverse)
    back = exchange(back.reshape(GX, ROWS, 128), "gx").reshape(GX * ROWS, 128)
    out = final_stage(field, back, depth_table(), bypass_weight, bypass_bias)
    return out.reshape(1, C, RX, RY, ZT)


def solution(mesh):
    in_specs = (P(None, None, "gx", "gy", None), P(None, None, None, ("gx", "gy")), P(), P())
    out_specs = P(None, None, "gx", "gy", None)
    return jax.shard_map(shards, mesh=mesh, in_specs=in_specs, out_specs=out_specs, check_vma=False)
```
